512 devices in a mesh: roll: 32 (over x, y_lo, core), head: 16 (over z, y_hi).
Axes of the slice: x: 4, y: 8 (y_hi: 2, y_lo: 4; y = y_hi * 4 + y_lo), z: 8, core: 2. Of those that a mesh axis runs over, the one named last changes fastest.
Arguments:
- hidden: bfloat16 [32, 256, 5376], P('roll', 'head'), may hold values from -6 to 6
- in_gain: float32 [5376], replicated, may hold values from 0.1 to 1.9
- w_query: bfloat16 [5376, 4096], P('roll', 'head'), may hold values from -0.078125 to 0.078125
- w_key: bfloat16 [5376, 2048], P('roll', 'head'), may hold values from -0.078125 to 0.078125
- w_value: bfloat16 [5376, 2048], P('roll', 'head'), may hold values from -0.078125 to 0.078125
- q_gain: float32 [128], replicated, may hold values from 0.1 to 1.9
- k_gain: float32 [128], replicated, may hold values from 1 to 5
- w_out: bfloat16 [4096, 5376], P('head', 'roll'), may hold values from -0.09375 to 0.09375
- out_gain: float32 [5376], replicated, may hold values from 0.1 to 1.9
- cache_keys: bfloat16 [5120, 2048], P('roll', 'head'), may hold values from -160 to 160
- cache_values: bfloat16 [5120, 2048], P('roll', 'head'), may hold values from -6 to 6
- block_table: int32 [32], replicated, may hold values from 0 to 31, each once
- seg_length: int32 [32], P('roll'), may hold values from 1 to 256, 5120 in all
- tool_mask: int32 [32, 256], P('roll', 'head'), may hold values 0 or 1
Outputs:
- layer_out: bfloat16 [32, 256, 5376], P('roll', 'head')
The draws below stay inside these ranges and needn't reach their ends.
Inputs may be any that keep to these rules, and one draw needn't show every extreme that they name: `block_table`: each slot's prompt block; every block is held by exactly one slot. `seg_length`: some rollout has all 256 slots present.
All inputs are finite; a program needn't handle non-finite values. No bound on the sum of `seg_length` or of `tool_mask` on one device may be relied on, other than what follows from the above.
Results may differ from the reference program's by a relative error of at most 0.018.
The reference program's roundings to bfloat16 on the way count: a program that leaves them out, or rounds other values in their place, can miss the bound.
Values may be sent and summed in bfloat16 or wider, within the bound.
A program may use at most 64 MiB of HBM per device.

```python
import math
import jax
import jax.numpy as jnp
import numpy as np
from jax import lax

D = 5376
HD = 128
QH = 32
KVH = 16
QSCALE = 168
SEG = 256
ROLLS = 32
PROMPT = 5120
N_ROLL = 32
N_HEAD = 16


def draw_cache_keys(key, part):
    key = jax.random.fold_in(key, 7)
    entries = jnp.clip(jax.random.normal(key, (PROMPT, KVH * HD), jnp.float32), -4.0, 4.0)
    return entries.astype(jnp.bfloat16)


def place_ends(array, rng, least, high):
    shape = array.shape
    spot = [jax.random.randint(jax.random.fold_in(rng, axis), (), 0, shape[axis]) for axis in range(len(shape))]
    array = array.at[tuple(spot)].set(least)
    longest = shape.index(max(shape))
    spot[longest] = (spot[longest] + 1) % shape[longest]
    return array.at[tuple(spot)].set(high)


def level_of(rng, extent, cuts, least, largest):
    level = 1.0
    for axis_at, blocks in cuts:
        heights = jax.random.uniform(jax.random.fold_in(jax.random.fold_in(rng, 6), axis_at), (blocks,), jnp.float32, least / len(cuts), largest / len(cuts))
        level = level * jnp.repeat(jnp.exp(heights), extent[axis_at] // blocks).reshape((-1,) + (1,) * (len(extent) - 1 - axis_at))
    return level


def profile(number_of, total, most, lean):
    portions = [(1 << 20) // math.isqrt(rank ** lean) + 1 for rank in range(2, number_of + 1)]
    spare, given = total - most - (number_of - 1), [1] * (number_of - 1)
    while spare > 0:
        candidates = [i for i in range(number_of - 1) if given[i] < most]
        mass, budget = sum([portions[i] for i in candidates]), spare
        for i in candidates:
            more = min(most - given[i], max(1, budget * portions[i] // mass), spare)
            given[i] = given[i] + more
            spare = spare - more
    return np.array([most] + given)


def uneven(rng, amount, total, reach, slope):
    if amount == 2:
        one = jax.random.randint(rng, (), max(1, total - reach), min(reach, total - 1) + 1)
        return jnp.stack([one, total - one])
    sizes = jnp.asarray(profile(amount, total, reach, slope), jnp.int32)
    pairs = (amount - 1) // 2
    giver, sink = sizes[1:1 + 2 * pairs:2], sizes[2:2 + 2 * pairs:2]
    margin = jnp.minimum(giver - 1, reach - sink)
    shifted = jax.random.randint(jax.random.fold_in(rng, 1), (pairs,), 0, 1 << 20) % (margin + 1)
    sizes = sizes.at[1:1 + 2 * pairs:2].set(giver - shifted).at[2:2 + 2 * pairs:2].set(sink + shifted)
    return sizes[jax.random.permutation(jax.random.fold_in(rng, 2), amount)]


def scatter_about(stream_key, shape, deviation, reach, split=(), kind=jnp.bfloat16):
    values = jax.random.normal(stream_key, shape, jnp.float32) * deviation
    if len(split) > 0:
        values = level_of(stream_key, shape, split, -0.22, 0.18) * values
    return jnp.clip(values, min=-reach, max=reach).astype(kind)


def setup_inputs(seed: int = 0) -> dict:
    splits = jax.random.split(jax.random.key(seed), 15)
    hidden = scatter_about(splits[0], (ROLLS, SEG, D), 1.0, 6.0, ((0, 32), (1, 16)))
    in_gain = jnp.clip(1.0 + 0.18 * jax.random.normal(splits[1], (D,), jnp.float32), 0.1, 1.9)
    w_query = scatter_about(splits[2], (D, QH * HD), D ** -0.5, 0.078125, ((0, 32), (1, 16)))
    w_key = scatter_about(splits[3], (D, KVH * HD), D ** -0.5, 0.078125, ((0, 32), (1, 16)))
    w_value = scatter_about(splits[4], (D, KVH * HD), D ** -0.5, 0.078125, ((0, 32), (1, 16)))
    q_gain = jnp.clip(1.0 + 0.18 * jax.random.normal(splits[5], (HD,), jnp.float32), 0.1, 1.9)
    k_gain = jnp.clip(jnp.exp(jax.random.uniform(splits[6], (HD,), jnp.float32, math.log(1.0), math.log(5.0))), 1.0, 5.0)
    w_out = scatter_about(splits[7], (QH * HD, D), (QH * HD) ** -0.5, 0.09375, ((0, 16), (1, 32)))
    out_gain = jnp.clip(1.0 + 0.18 * jax.random.normal(splits[8], (D,), jnp.float32), 0.1, 1.9)
    cache_keys = draw_cache_keys(jax.random.fold_in(splits[14], 71), 0)
    cache_values = scatter_about(splits[10], (PROMPT, KVH * HD), 1.0, 6.0, ((0, 32), (1, 16)))
    block_table = jax.random.permutation(splits[11], N_ROLL).astype(jnp.int32)
    seg_length = uneven(splits[12], ROLLS, ROLLS * SEG * 5 // 8, SEG, 1).astype(jnp.int32)
    tool_mask = place_ends((jax.random.randint(splits[13], (ROLLS, SEG), 0, 4) < 1).astype(jnp.int32), jax.random.fold_in(splits[13], 1), 0, 1)
    return {"hidden": hidden, "in_gain": in_gain, "w_query": w_query, "w_key": w_key, "w_value": w_value, "q_gain": q_gain, "k_gain": k_gain, "w_out": w_out, "out_gain": out_gain, "cache_keys": cache_keys, "cache_values": cache_values, "block_table": block_table, "seg_length": seg_length, "tool_mask": tool_mask}


epsilon = 1e-06
rope_base = 1000000.0

def rms_scale(values, gain_row):
    mean_square = lax.optimization_barrier(jnp.mean(values * values, axis=-1, keepdims=True))
    return values * lax.rsqrt(mean_square + epsilon) * gain_row

def rotate(values, positions):
    half_size = values.shape[-1] // 2
    inverse = rope_base ** (-jnp.arange(half_size, dtype=jnp.float32) * 2.0 / values.shape[-1])
    angles = positions.astype(jnp.float32)[:, None] * inverse[None, :]
    cosine_table = jnp.cos(angles)[:, None, :]
    sine_table = jnp.sin(angles)[:, None, :]
    first_half = values[..., :half_size]
    second_half = values[..., half_size:]
    return jnp.concatenate([first_half * cosine_table - second_half * sine_table, second_half * cosine_table + first_half * sine_table], axis=-1)

def reference(hidden, in_gain, w_query, w_key, w_value, q_gain, k_gain, w_out, out_gain, cache_keys, cache_values, block_table, seg_length, tool_mask):
    head_dim = q_gain.shape[0]
    kv_heads = w_key.shape[1] // head_dim
    q_heads = w_query.shape[1] // head_dim
    group_size = q_heads // kv_heads
    prompt_rows = cache_keys.shape[0]
    block_rows = prompt_rows // N_ROLL
    seg_rows = hidden.shape[1]
    row_ids = jnp.arange(prompt_rows, dtype=jnp.int32)
    prompt_pos = block_table[row_ids // block_rows] * block_rows + row_ids % block_rows
    prompt_keys = rotate(cache_keys.astype(jnp.float32).reshape(prompt_rows, kv_heads, head_dim), prompt_pos).astype(jnp.bfloat16)
    prompt_values = cache_values.reshape(prompt_rows, kv_heads, head_dim)
    seg_pos = prompt_rows + jnp.arange(seg_rows, dtype=jnp.int32)
    token_ids = jnp.arange(seg_rows, dtype=jnp.int32)
    causal = token_ids[None, :] <= token_ids[:, None]
    group_cols = q_heads * head_dim // N_HEAD
    score_scale = 1.0 / QSCALE ** 0.5

    def one_rollout(inputs_row):
        tokens, length, tool_row = inputs_row
        normed = rms_scale(tokens.astype(jnp.float32), in_gain).astype(jnp.bfloat16)
        proj_query = jnp.dot(normed, w_query, preferred_element_type=jnp.float32).reshape(seg_rows, q_heads, head_dim)
        seg_queries = rotate(rms_scale(proj_query, q_gain), seg_pos).astype(jnp.bfloat16)
        proj_key = jnp.dot(normed, w_key, preferred_element_type=jnp.float32).reshape(seg_rows, kv_heads, head_dim)
        seg_keys = rotate(rms_scale(proj_key, k_gain), seg_pos).astype(jnp.bfloat16)
        seg_values = jnp.dot(normed, w_value, preferred_element_type=jnp.float32).astype(jnp.bfloat16).reshape(seg_rows, kv_heads, head_dim)
        keys_all = jnp.concatenate([prompt_keys, seg_keys], axis=0).astype(jnp.float32)
        values_all = jnp.concatenate([prompt_values, seg_values], axis=0).astype(jnp.float32)
        grouped = seg_queries.astype(jnp.float32).reshape(seg_rows, kv_heads, group_size, head_dim)
        scores = jnp.einsum('tgrd,ngd->grtn', grouped, keys_all) * score_scale
        live_mask = causal & (token_ids[None, :] < length)
        visible = jnp.concatenate([jnp.ones((seg_rows, prompt_rows), dtype=bool), live_mask], axis=1)
        scores = jnp.where(visible, scores, -jnp.inf)
        probs = jax.nn.softmax(scores, axis=-1).astype(jnp.bfloat16)
        combined = jnp.einsum('grtn,ngd->tgrd', probs.astype(jnp.float32), values_all, precision=lax.Precision.HIGHEST)
        attended = combined.reshape(seg_rows, q_heads * head_dim).astype(jnp.bfloat16)
        proj_sum = jnp.zeros((seg_rows, w_out.shape[1]), jnp.float32)
        for group_index in range(N_HEAD):
            lower = group_index * group_cols
            term = jnp.dot(attended[:, lower:lower + group_cols], w_out[lower:lower + group_cols], preferred_element_type=jnp.float32).astype(jnp.bfloat16)
            term = lax.optimization_barrier(term)
            proj_sum = proj_sum + term.astype(jnp.float32)
        branch = rms_scale(proj_sum, out_gain)
        keep_rows = ((token_ids < length) & (tool_row == 0)).astype(jnp.float32)[:, None]
        return ((tokens.astype(jnp.float32) + branch) * keep_rows).astype(jnp.bfloat16)
    return lax.map(one_rollout, (hidden, seg_length, tool_mask))
```

```python
import functools

import jax
import jax.numpy as jnp
import numpy as np
from jax import lax
from jax.experimental import pallas as pl
from jax.experimental.pallas import tpu as pltpu
from jax.sharding import PartitionSpec as P

QSCALE = 168
EPSILON = 1e-06
ROPE_BASE = 1000000.0
MESH = pl.DeviceIdType.MESH
F32 = jnp.float32
BF16 = jnp.bfloat16

NX, NY, NC, NZ, NH = 4, 4, 2, 8, 2
PIECES = 6


def rope_rows(positions, head_dim):
    half = head_dim // 2
    inverse = ROPE_BASE ** (-np.arange(half, dtype=np.float64) * 2.0 / head_dim)
    angles = np.asarray(positions, np.float64)[:, None] * inverse[None, :]
    cosine, sine = np.cos(angles), np.sin(angles)
    return (
        np.concatenate([cosine, cosine], axis=1).astype(np.float32),
        np.concatenate([-sine, sine], axis=1).astype(np.float32),
    )


def unit_rms(values):
    mean_square = jnp.mean(values * values, axis=-1, keepdims=True)
    return values * lax.rsqrt(mean_square + EPSILON)


def rotate(values, cosine, signed_sine):
    half = values.shape[-1] // 2
    return values * cosine + pltpu.roll(values, half, axis=1) * signed_sine


def nt_dot(left, right):
    return lax.dot_general(left, right, (((1,), (1,)), ((), ())), preferred_element_type=F32)


def kernel(
    hid, ing, wq, wk, wv, qg, kg, wo, og, ck, cv,
    block_cos, block_sin, row_cos, row_sin, seg_cos, seg_sin,
    table, length_ref, tool,
    out,
    tok, wb, kvb, wob, wsrc, wst, osrc, ost, term, ru, rd, ysend, yrecv, total,
    proj, queries, att_acc, row_best, row_total,
    send_sems, recv_sems,
):
    roll, head = lax.axis_index("roll"), lax.axis_index("head")
    x, yl, c = lax.div(roll, 8), lax.rem(lax.div(roll, 2), 4), lax.rem(roll, 2)
    z, yh = lax.div(head, 2), lax.rem(head, 2)
    own_rows, width = hid.shape
    slots, shard = table.shape[0], wq.shape[0]
    pair = 2 * shard
    block_rows = ck.shape[0]
    hd = qg.shape[1]
    seg = tok.shape[0]
    half_width = width // 2
    piece = width // PIECES

    def wrap(value, size):
        return lax.rem(value + size, size)

    def dev(x_=x, yl_=yl, c_=c, z_=z, yh_=yh):
        return {"roll": (x_ * NY + yl_) * NC + c_, "head": z_ * NH + yh_}

    sibling = dev(c_=1 - c)
    x_up, x_down = dev(x_=wrap(x + 1, NX)), dev(x_=wrap(x - 1, NX))
    z_up, z_down = dev(z_=wrap(z + 1, NZ)), dev(z_=wrap(z - 1, NZ))
    y_others = [dev(yl_=wrap(yl + j, NY)) for j in range(1, NY)]
    partner = dev(yh_=1 - yh)

    index_of = {}
    started = []

    def slot_of(key):
        return index_of.setdefault(key, len(index_of))

    def copy_of(key, src, dst, where):
        i = slot_of(key)
        return pltpu.make_async_remote_copy(
            src_ref=src, dst_ref=dst, send_sem=send_sems.at[i], recv_sem=recv_sems.at[i],
            device_id=where, device_id_type=MESH,
        )

    def send(key, src, where, dst=None):
        copy = copy_of(key, src, src if dst is None else dst, where)
        copy.start()
        started.append(copy)

    def recv(key, dst):
        copy_of(key, dst, dst, sibling).wait_recv()

    barrier = pltpu.get_barrier_semaphore()
    for where in [sibling, x_up, x_down, z_up, z_down, partner] + y_others:
        pl.semaphore_signal(barrier, inc=1, device_id=where, device_id_type=MESH)
    pl.semaphore_wait(barrier, 6 + len(y_others))

    wsrc[0] = wq[...]
    wsrc[1, :, 0:hd] = wk[...]
    wsrc[1, :, hd : 2 * hd] = wv[...]
    send("W sibling", wsrc.at[1 - c], sibling, wst)

    def token_block(zz, yy, part):
        return tok.at[
            pl.ds(pl.multiple_of((zz * NH + yy) * own_rows, own_rows), own_rows),
            pl.ds(part * half_width, half_width),
        ]

    def token_key(group, way, distance, part):
        return ("T", group, way, distance, part)

    def token_own(group):
        yy = yh if group == 0 else 1 - yh
        for part in range(2):
            if group == 1:
                recv(("TP", part), token_block(z, yy, part))
            block = token_block(z, yy, part)
            send(token_key(group, "u", 1, part), block, z_up)
            send(token_key(group, "d", 1, part), block, z_down)

    def token_step(group, distance):
        yy = yh if group == 0 else 1 - yh
        for part in range(2):
            for way, sign, where in (("u", -1, z_up), ("d", 1, z_down)):
                if distance == 4 and part != (0 if way == "u" else 1):
                    continue
                block = token_block(wrap(z + sign * distance, NZ), yy, part)
                recv(token_key(group, way, distance, part), block)
                if distance < 3 or (distance == 3 and part == (0 if way == "u" else 1)):
                    send(token_key(group, way, distance + 1, part), block, where)

    normed = unit_rms(hid[...].astype(F32)) * ing[...]
    tok[pl.ds(pl.multiple_of(head * own_rows, own_rows), own_rows), :] = normed.astype(BF16)
    token_own(0)
    for part in range(2):
        send(("TP", part), token_block(z, yh, part), partner)

    class Gather:
        def __init__(self, name, block, part):
            self.name, self.block, self.part = name, block, part

        def at(self, dx, i, core):
            return self.block(wrap(x + dx, NX), wrap(yl - i, NY), core)

        def half(self, dx, i, k):
            return self.part(wrap(x + dx, NX), wrap(yl - i, NY), c, k)

        def own(self):
            block = self.at(0, 0, c)
            send((self.name, "u", 0), block, x_up)
            send((self.name, "d", 0), block, x_down)
            for j in range(1, NY):
                send((self.name, "y", j), block, y_others[j - 1])
            send((self.name, "s", 0, 0), block, sibling)

        def y_step(self, i):
            block = self.at(0, i, c)
            recv((self.name, "y", i), block)
            send((self.name, "u", i), block, x_up)
            send((self.name, "d", i), block, x_down)
            send((self.name, "s", 0, i), block, sibling)

        def x_step(self, i):
            block = self.at(-1, i, c)
            recv((self.name, "u", i), block)
            send((self.name, "ou", i), self.half(-1, i, 0), x_up)
            send((self.name, "s", -1, i), block, sibling)
            block = self.at(1, i, c)
            recv((self.name, "d", i), block)
            send((self.name, "od", i), self.half(1, i, 1), x_down)
            send((self.name, "s", 1, i), block, sibling)

        def o_step(self, i):
            recv((self.name, "ou", i), self.half(2, i, 0))
            recv((self.name, "od", i), self.half(2, i, 1))
            send((self.name, "s", 2, i), self.at(2, i, c), sibling)

        def arrived(self, dx):
            for i in range(NY):
                recv((self.name, "s", dx, i), self.at(dx, i, 1 - c))

    first = 176

    def w_part(ref, core, chip, k):
        start, size = (0, first) if k == 0 else (first, pair - first)
        return ref.at[core, pl.ds(pl.multiple_of(chip * pair + start, 16), size)]

    def w_whole(ref, core, chip):
        return ref.at[core, pl.ds(pl.multiple_of(chip * pair, 16), pair)]

    def c_rows(chip, core, start, size):
        return kvb.at[pl.ds(pl.multiple_of((chip * NC + core) * block_rows + start, 16), size)]

    gather_w = Gather(
        "W",
        lambda xx, yy, core: w_whole(wb, core, xx * NY + yy),
        lambda xx, yy, core, k: w_part(wb, core, xx * NY + yy, k),
    )
    gather_c = Gather(
        "C",
        lambda xx, yy, core: c_rows(xx * NY + yy, core, 0, block_rows),
        lambda xx, yy, core, k: c_rows(xx * NY + yy, core, k * (block_rows // 2), block_rows // 2),
    )
    gather_o = Gather(
        "O",
        lambda xx, yy, core: w_whole(wob, core, xx * NY + yy),
        lambda xx, yy, core, k: w_part(wob, core, xx * NY + yy, k),
    )
    chip = x * NY + yl

    def join_pair(mine, other):
        mine, other = mine.astype(F32), other.astype(F32)
        upper = jnp.where(c == 0, mine, other)
        lower = jnp.where(c == 0, other, mine)
        return jnp.concatenate([upper, lower], axis=0).astype(BF16)

    recv("W sibling", wst)
    wb[c, pl.ds(pl.multiple_of(chip * pair, 16), pair), :] = join_pair(wsrc[c], wst[...])
    gather_w.own()

    slot_block = table[roll]
    pick = lax.broadcasted_iota(jnp.int32, (slots, hd), 0) == slot_block
    start_cos = jnp.sum(jnp.where(pick, block_cos[...], 0.0), axis=0, keepdims=True)
    start_sin = jnp.sum(jnp.where(pick, block_sin[...], 0.0), axis=0, keepdims=True)
    lane = lax.broadcasted_iota(jnp.int32, (1, hd), 1)
    sign = jnp.where(lane < hd // 2, -1.0, 1.0)
    cosine = start_cos * row_cos[...] - start_sin * row_sin[...]
    sine = (start_sin * row_cos[...] + start_cos * row_sin[...]) * sign
    own_cache = pl.ds(pl.multiple_of(roll * block_rows, 16), block_rows)
    kvb[own_cache, 0:hd] = rotate(ck[...].astype(F32), cosine, sine).astype(BF16)
    kvb[own_cache, hd : 2 * hd] = cv[...]

    rows_i = lax.broadcasted_iota(jnp.int32, (2 * hd, 2 * hd), 0)
    cols_i = lax.broadcasted_iota(jnp.int32, (2 * hd, 2 * hd), 1)
    identity = jnp.where(rows_i == cols_i, 1.0, 0.0).astype(BF16)
    turned = lax.dot_general(
        wo[...], identity, (((0,), (0,)), ((), ())), preferred_element_type=F32
    ).astype(BF16)
    osrc[0] = turned[:, 0:hd]
    osrc[1] = turned[:, hd : 2 * hd]
    send("O sibling", osrc.at[1 - c], sibling, ost)

    token_step(0, 1)
    gather_w.y_step(1)
    gather_w.y_step(2)
    token_step(0, 2)
    gather_w.y_step(3)
    token_own(1)
    token_step(0, 3)
    gather_w.x_step(0)
    gather_c.own()
    token_step(0, 4)
    token_step(1, 1)
    gather_w.x_step(1)
    gather_c.y_step(1)
    gather_w.x_step(2)
    gather_c.y_step(2)
    token_step(1, 2)
    gather_w.x_step(3)
    gather_c.y_step(3)
    recv("O sibling", ost)
    wob[c, pl.ds(pl.multiple_of(chip * pair, 16), pair), :] = join_pair(osrc[c], ost[...])
    gather_o.own()
    for i in range(NY):
        gather_w.o_step(i)
        gather_c.x_step(i)
    token_step(1, 3)
    for i in range(1, NY):
        gather_o.y_step(i)
    token_step(1, 4)
    for dx in (0, -1, 1, 2):
        gather_w.arrived(dx)

    depth = 768
    proj[...] = jnp.zeros_like(proj)

    def project(step, carry):
        at = pl.ds(pl.multiple_of(step * depth, depth), depth)
        rows = tok[:, at]
        proj[:, 0 : 2 * hd] += jnp.dot(rows, wb[0, at, :], preferred_element_type=F32)
        proj[:, 2 * hd : 4 * hd] += jnp.dot(rows, wb[1, at, :], preferred_element_type=F32)
        return carry

    lax.fori_loop(0, width // depth, project, 0)
    for g in range(2):
        query = unit_rms(proj[:, g * hd : (g + 1) * hd]) * qg[...]
        queries[pl.ds(g * seg, seg), :] = rotate(query, seg_cos[...], seg_sin[...]).astype(BF16)
    key = unit_rms(proj[:, 2 * hd : 3 * hd]) * kg[...]
    seg_key = rotate(key, seg_cos[...], seg_sin[...]).astype(BF16)
    seg_value = proj[:, 3 * hd : 4 * hd].astype(BF16)

    for i in range(NY):
        gather_c.o_step(i)
        gather_o.x_step(i)

    scale = 1.0 / QSCALE**0.5
    length = length_ref[0]
    scores = nt_dot(queries[...], seg_key) * scale
    row_t = lax.rem(lax.broadcasted_iota(jnp.int32, scores.shape, 0), seg)
    col_t = lax.broadcasted_iota(jnp.int32, scores.shape, 1)
    scores = jnp.where((col_t <= row_t) & (col_t < length), scores, -1e30)
    best = jnp.max(scores, axis=1, keepdims=True)
    weights = jnp.exp(scores - best)
    row_best[...] = jnp.broadcast_to(best, row_best.shape)
    row_total[...] = jnp.broadcast_to(jnp.sum(weights, axis=1, keepdims=True), row_total.shape)
    att_acc[...] = jnp.dot(weights.astype(BF16), seg_value, preferred_element_type=F32)

    keys_per = 640
    group_rows = NY * NC * block_rows

    for dx in (0, -1, 1, 2):
        gather_c.arrived(dx)
        group_start = wrap(x + dx, NX) * group_rows

        def attend(step, carry, group_start=group_start):
            at = pl.ds(pl.multiple_of(group_start + step * keys_per, 16), keys_per)
            scores = nt_dot(queries[...], kvb[at, 0:hd]) * scale
            old_best = row_best[:, 0:1]
            best = jnp.maximum(old_best, jnp.max(scores, axis=1, keepdims=True))
            rescale = jnp.exp(old_best - best)
            weights = jnp.exp(scores - best)
            row_best[...] = jnp.broadcast_to(best, row_best.shape)
            row_total[...] = row_total[...] * rescale + jnp.sum(weights, axis=1, keepdims=True)
            att_acc[...] = att_acc[...] * rescale + jnp.dot(
                weights.astype(BF16), kvb[at, hd : 2 * hd], preferred_element_type=F32
            )
            return carry

        lax.fori_loop(0, group_rows // keys_per, attend, 0)

    for i in range(NY):
        gather_o.o_step(i)
    combined = (att_acc[...] / row_total[...]).astype(BF16)
    attended = jnp.concatenate([combined[0:seg], combined[seg : 2 * seg]], axis=1)
    for dx in (0, -1, 1, 2):
        gather_o.arrived(dx)

    span = NH * own_rows

    def term_at(dz, p):
        return (
            pl.ds(pl.multiple_of(wrap(z + dz, NZ) * span, span), span),
            pl.ds(p * piece, piece),
        )

    def make_term(p):
        at = pl.ds(p * piece, piece)
        columns = jnp.concatenate([wob[0, at, :], wob[1, at, :]], axis=1)
        term[:, at] = nt_dot(attended, columns).astype(BF16)

    def ring_step(way, k, p):
        sign, where, buf = (1, z_up, ru) if way == "u" else (-1, z_down, rd)
        at = term_at(sign * (4 - k), p)
        first_piece = (p < PIECES // 2) == (way == "u")
        if k >= 2 or (k == 1 and first_piece):
            recv(("R", way, k - 1, p), buf.at[k - 1, p])
            term[at] = (term[at].astype(F32) + buf[k - 1, p].astype(F32)).astype(BF16)
        send(("R", way, k, p), term.at[at], where, buf.at[k, p])

    up_first, down_first = [0, 1, 2], [3, 4, 5]
    for pu, pd in zip(up_first, down_first):
        make_term(pu)
        ring_step("u", 0, pu)
        make_term(pd)
        ring_step("d", 0, pd)
    for pu, pd in zip(down_first, up_first):
        ring_step("u", 1, pu)
        ring_step("d", 1, pd)
    for pu, pd in zip(up_first, down_first):
        ring_step("u", 1, pu)
        ring_step("d", 1, pd)
    for k in (2, 3):
        for pu, pd in zip(down_first + up_first, up_first + down_first):
            ring_step("u", k, pu)
            ring_step("d", k, pd)
    for p in (0, 3, 1, 4, 2, 5):
        recv(("R", "u", 3, p), ru.at[3, p])
        recv(("R", "d", 3, p), rd.at[3, p])
        at = pl.ds(p * piece, piece)
        total[:, at] = (
            term[term_at(0, p)].astype(F32) + ru[3, p].astype(F32) + rd[3, p].astype(F32)
        )
        theirs = pl.ds(pl.multiple_of((1 - yh) * own_rows, own_rows), own_rows)
        ysend[p] = total[theirs, at].astype(BF16)
        send(("Y", p), ysend.at[p], partner, yrecv.at[p])
    mine = pl.ds(pl.multiple_of(yh * own_rows, own_rows), own_rows)
    sums = []
    for p in range(PIECES):
        recv(("Y", p), yrecv.at[p])
        sums.append(total[mine, pl.ds(p * piece, piece)] + yrecv[p].astype(F32))
    branch = unit_rms(jnp.concatenate(sums, axis=1)) * og[...]
    row_i = lax.broadcasted_iota(jnp.int32, (own_rows, 1), 0)
    masked = jnp.zeros((own_rows, 1), jnp.int32)
    for t in range(own_rows):
        masked = jnp.where(row_i == t, tool[0, t], masked)
    keep = jnp.where((head * own_rows + row_i < length) & (masked == 0), 1.0, 0.0)
    out[...] = ((hid[...].astype(F32) + branch) * keep).astype(BF16)

    for copy in started:
        copy.wait_send()


def on_device(
    hidden, in_gain, w_query, w_key, w_value, q_gain, k_gain, w_out, out_gain,
    cache_keys, cache_values, block_table, seg_length, tool_mask,
):
    own_rows, width = hidden.shape[1:]
    hd = q_gain.shape[0]
    slots = block_table.shape[0]
    block_rows = cache_keys.shape[0]
    seg = own_rows * NZ * NH
    shard = w_query.shape[0]
    half = hd // 2
    block_cos, block_sin = rope_rows(np.arange(slots) * block_rows, hd)
    row_cos, row_sin = rope_rows(np.arange(block_rows), hd)
    block_sin = np.concatenate([block_sin[:, half:], block_sin[:, half:]], axis=1)
    row_sin = np.concatenate([row_sin[:, half:], row_sin[:, half:]], axis=1)
    seg_cos, seg_sin = rope_rows(slots * block_rows + np.arange(seg), hd)
    piece = width // PIECES
    span = NH * own_rows
    vmem = pl.BlockSpec(memory_space=pltpu.VMEM)
    smem = pl.BlockSpec(memory_space=pltpu.SMEM)
    copies = 200
    result = pl.pallas_call(
        kernel,
        out_shape=jax.ShapeDtypeStruct((own_rows, width), BF16),
        in_specs=[vmem] * 17 + [smem] * 3,
        out_specs=vmem,
        scratch_shapes=[
            pltpu.VMEM((seg, width), BF16),
            pltpu.VMEM((2, width, 2 * hd), BF16),
            pltpu.VMEM((slots * block_rows, 2 * hd), BF16),
            pltpu.VMEM((2, width, hd), BF16),
            pltpu.VMEM((2, shard, 2 * hd), BF16),
            pltpu.VMEM((shard, 2 * hd), BF16),
            pltpu.VMEM((2, shard, hd), BF16),
            pltpu.VMEM((shard, hd), BF16),
            pltpu.VMEM((seg, width), BF16),
            pltpu.VMEM((4, PIECES, span, piece), BF16),
            pltpu.VMEM((4, PIECES, span, piece), BF16),
            pltpu.VMEM((PIECES, own_rows, piece), BF16),
            pltpu.VMEM((PIECES, own_rows, piece), BF16),
            pltpu.VMEM((span, width), F32),
            pltpu.VMEM((seg, 4 * hd), F32),
            pltpu.VMEM((2 * seg, hd), BF16),
            pltpu.VMEM((2 * seg, hd), F32),
            pltpu.VMEM((2 * seg, hd), F32),
            pltpu.VMEM((2 * seg, hd), F32),
            pltpu.SemaphoreType.DMA((copies,)),
            pltpu.SemaphoreType.DMA((copies,)),
        ],
        compiler_params=pltpu.CompilerParams(
            collective_id=0, has_side_effects=True, vmem_limit_bytes=56 * 2**20
        ),
    )(
        hidden[0], in_gain[None], w_query, w_key, w_value, q_gain[None], k_gain[None], w_out,
        out_gain[None], cache_keys, cache_values,
        block_cos, block_sin, row_cos, row_sin, seg_cos, seg_sin,
        block_table, seg_length, tool_mask,
    )
    return result[None]


def solution(mesh):
    return jax.shard_map(
        on_device,
        mesh=mesh,
        in_specs=(
            P("roll", "head", None),
            P(),
            P("roll", "head"),
            P("roll", "head"),
            P("roll", "head"),
            P(),
            P(),
            P("head", "roll"),
            P(),
            P("roll", "head"),
            P("roll", "head"),
            P(),
            P("roll"),
            P("roll", "head"),
        ),
        out_specs=P("roll", "head", None),
        check_vma=False,
    )
```

```python
import math

import jax
import jax.numpy as jnp
import numpy as np
from jax import lax
from jax.experimental import pallas as pl
from jax.experimental.pallas import tpu as pltpu
from jax.sharding import PartitionSpec as P

QSCALE = 168
EPSILON = 1e-06
ROPE_BASE = 1000000.0
MESH = pl.DeviceIdType.MESH
F32 = jnp.float32
BF16 = jnp.bfloat16

NX, NY, NC, NZ, NH = 4, 4, 2, 8, 2
PIECES = 6

(
    TOKENS, TOKENS_OWN, READY, PROJECT, SEGMENT, ATTEND, CLOSE, TERM, RING, LAST, FINISH,
    OWN_Y, OWN_X, FROM_Y, FROM_X, FROM_OPPOSITE, ARRIVED,
) = range(17)
UP, DOWN = range(2)
QKV, CACHE, OUT = range(3)
ORDER = (
    (OWN_Y, CACHE, 0), (TOKENS, 0, DOWN, 1, 0), (OWN_X, CACHE, 0), (FROM_Y, QKV, 1, 0),
    (TOKENS, 0, UP, 1, 1), (FROM_X, QKV, DOWN, 0, 1), (FROM_Y, QKV, 1, 1),
    (FROM_X, CACHE, DOWN, 0, 0), (TOKENS, 0, UP, 2, 1), (READY,), (OWN_X, OUT, 0),
    (FROM_X, QKV, UP, 1, 0), (FROM_Y, CACHE, 1, 0), (OWN_Y, CACHE, 1), (FROM_X, QKV, UP, 0, 0),
    (TOKENS, 0, UP, 1, 0), (FROM_X, CACHE, UP, 0, 0), (OWN_X, OUT, 1), (TOKENS, 0, DOWN, 1, 1),
    (TOKENS, 0, DOWN, 2, 0), (OWN_X, CACHE, 1), (FROM_X, QKV, DOWN, 1, 1), (FROM_X, QKV, UP, 0, 1),
    (FROM_Y, QKV, 2, 1), (FROM_OPPOSITE, QKV, DOWN, 0), (TOKENS_OWN, 1), (FROM_Y, QKV, 2, 0),
    (FROM_X, QKV, DOWN, 1, 0), (FROM_Y, CACHE, 1, 1), (TOKENS, 0, DOWN, 2, 1), (FROM_Y, QKV, 3, 0),
    (OWN_Y, OUT, 1), (TOKENS, 1, UP, 1, 0), (TOKENS, 1, DOWN, 1, 1), (TOKENS, 0, UP, 2, 0),
    (FROM_X, CACHE, DOWN, 0, 1), (FROM_Y, QKV, 3, 1), (FROM_X, QKV, DOWN, 2, 1),
    (TOKENS, 1, UP, 1, 1), (FROM_Y, CACHE, 3, 0), (OWN_Y, OUT, 0), (TOKENS, 1, DOWN, 1, 0),
    (FROM_OPPOSITE, QKV, UP, 0), (FROM_Y, CACHE, 2, 1), (FROM_X, OUT, UP, 0, 1),
    (TOKENS, 0, DOWN, 3, 1), (TOKENS, 1, UP, 2, 0), (TOKENS, 1, DOWN, 2, 1), (FROM_Y, OUT, 1, 1),
    (FROM_X, QKV, UP, 2, 0), (FROM_Y, CACHE, 3, 1), (TOKENS, 0, UP, 3, 0), (TOKENS, 1, DOWN, 2, 0),
    (FROM_X, QKV, UP, 2, 1), (FROM_X, QKV, DOWN, 2, 0), (TOKENS, 1, UP, 2, 1),
    (FROM_X, QKV, UP, 3, 0), (FROM_X, QKV, DOWN, 3, 1), (TOKENS, 1, UP, 3, 0),
    (FROM_X, QKV, UP, 1, 1), (FROM_OPPOSITE, QKV, UP, 1), (TOKENS, 0, DOWN, 4, 1),
    (FROM_Y, OUT, 2, 1), (FROM_Y, OUT, 3, 1), (TOKENS, 1, DOWN, 3, 1), (FROM_Y, OUT, 1, 0),
    (FROM_X, QKV, UP, 3, 1), (FROM_Y, OUT, 2, 0), (FROM_Y, CACHE, 2, 0), (FROM_X, OUT, DOWN, 0, 1),
    (FROM_X, CACHE, DOWN, 2, 1), (FROM_X, CACHE, DOWN, 1, 1), (FROM_X, QKV, DOWN, 0, 0),
    (FROM_OPPOSITE, CACHE, DOWN, 0), (FROM_OPPOSITE, QKV, DOWN, 1), (FROM_X, OUT, UP, 1, 1),
    (ARRIVED, QKV, 0), (FROM_OPPOSITE, QKV, DOWN, 2), (FROM_X, CACHE, UP, 3, 0),
    (FROM_X, QKV, DOWN, 3, 0), (FROM_X, CACHE, UP, 1, 0), (TOKENS, 0, DOWN, 3, 0),
    (TOKENS, 0, UP, 4, 0), (FROM_X, CACHE, DOWN, 1, 0), (FROM_Y, OUT, 3, 0),
    (FROM_OPPOSITE, QKV, UP, 2), (FROM_OPPOSITE, QKV, DOWN, 3), (TOKENS, 0, UP, 3, 1),
    (FROM_X, CACHE, UP, 3, 1), (FROM_X, OUT, DOWN, 0, 0), (FROM_X, OUT, UP, 0, 0),
    (FROM_X, CACHE, UP, 0, 1), (FROM_OPPOSITE, QKV, UP, 3), (FROM_X, CACHE, UP, 2, 1),
    (FROM_X, OUT, DOWN, 1, 1), (TOKENS, 1, DOWN, 3, 0), (FROM_X, CACHE, DOWN, 3, 0),
    (ARRIVED, QKV, 1), (FROM_X, CACHE, UP, 1, 1), (TOKENS, 1, UP, 3, 1),
    (FROM_X, CACHE, DOWN, 3, 1), (ARRIVED, OUT, 0), (TOKENS, 1, UP, 4, 0), (FROM_X, OUT, UP, 2, 1),
    (ARRIVED, QKV, -1), (TOKENS, 1, DOWN, 4, 1), (ARRIVED, QKV, 2), (PROJECT,), (SEGMENT, 0),
    (ARRIVED, CACHE, 0), (FROM_X, OUT, UP, 1, 0), (FROM_X, CACHE, UP, 2, 0),
    (FROM_X, OUT, DOWN, 3, 1), (FROM_X, OUT, UP, 3, 1), (ATTEND, 0, 0), (FROM_X, OUT, DOWN, 2, 1),
    (FROM_OPPOSITE, CACHE, UP, 1), (FROM_X, OUT, DOWN, 1, 0), (FROM_OPPOSITE, CACHE, UP, 3),
    (FROM_X, OUT, DOWN, 2, 0), (FROM_X, OUT, UP, 2, 0), (ARRIVED, CACHE, -1),
    (FROM_OPPOSITE, CACHE, UP, 0), (FROM_X, OUT, UP, 3, 0), (FROM_X, CACHE, DOWN, 2, 0),
    (ATTEND, 0, -1), (FROM_OPPOSITE, CACHE, DOWN, 1), (FROM_X, OUT, DOWN, 3, 0),
    (FROM_OPPOSITE, OUT, DOWN, 1), (FROM_OPPOSITE, CACHE, DOWN, 2), (ARRIVED, CACHE, 1),
    (FROM_OPPOSITE, OUT, UP, 0), (FROM_OPPOSITE, CACHE, UP, 2), (ARRIVED, OUT, -1),
    (FROM_OPPOSITE, OUT, UP, 1), (FROM_OPPOSITE, OUT, DOWN, 0), (ARRIVED, OUT, 1),
    (FROM_OPPOSITE, CACHE, DOWN, 3), (ATTEND, 0, 1), (FROM_OPPOSITE, OUT, UP, 3),
    (FROM_OPPOSITE, OUT, UP, 2), (FROM_OPPOSITE, OUT, DOWN, 3), (ARRIVED, CACHE, 2),
    (FROM_OPPOSITE, OUT, DOWN, 2), (ATTEND, 0, 2), (ARRIVED, OUT, 2), (CLOSE, 0), (TERM, 0, 0),
    (RING, 0, UP, 0, 0), (TERM, 0, 3), (RING, 0, DOWN, 0, 3), (TERM, 0, 1), (RING, 0, UP, 0, 1),
    (TERM, 0, 4), (RING, 0, DOWN, 0, 4), (TERM, 0, 2), (RING, 0, UP, 0, 2), (TERM, 0, 5),
    (RING, 0, DOWN, 0, 5), (RING, 0, UP, 1, 3), (RING, 0, DOWN, 1, 0), (RING, 0, UP, 1, 4),
    (RING, 0, DOWN, 1, 1), (RING, 0, UP, 1, 5), (RING, 0, DOWN, 1, 2), (SEGMENT, 1), (ATTEND, 1, 0),
    (RING, 0, UP, 1, 0), (RING, 0, DOWN, 1, 3), (RING, 0, UP, 1, 1), (RING, 0, DOWN, 1, 4),
    (RING, 0, UP, 1, 2), (RING, 0, DOWN, 1, 5), (ATTEND, 1, -1), (ATTEND, 1, 1),
    (RING, 0, UP, 2, 3), (RING, 0, DOWN, 2, 0), (RING, 0, UP, 2, 4), (RING, 0, DOWN, 2, 1),
    (RING, 0, UP, 2, 5), (RING, 0, DOWN, 2, 2), (RING, 0, UP, 2, 0), (RING, 0, DOWN, 2, 3),
    (RING, 0, UP, 2, 1), (RING, 0, DOWN, 2, 4), (RING, 0, UP, 2, 2), (RING, 0, DOWN, 2, 5),
    (ATTEND, 1, 2), (CLOSE, 1), (RING, 0, UP, 3, 3), (RING, 0, DOWN, 3, 0), (RING, 0, UP, 3, 4),
    (RING, 0, DOWN, 3, 1), (RING, 0, UP, 3, 5), (RING, 0, DOWN, 3, 2), (RING, 0, UP, 3, 0),
    (RING, 0, DOWN, 3, 3), (RING, 0, UP, 3, 1), (RING, 0, DOWN, 3, 4), (RING, 0, UP, 3, 2),
    (RING, 0, DOWN, 3, 5), (TERM, 1, 0), (RING, 1, UP, 0, 0), (TERM, 1, 3), (RING, 1, DOWN, 0, 3),
    (TERM, 1, 1), (RING, 1, UP, 0, 1), (TERM, 1, 4), (RING, 1, DOWN, 0, 4), (TERM, 1, 2),
    (RING, 1, UP, 0, 2), (TERM, 1, 5), (RING, 1, DOWN, 0, 5), (RING, 1, UP, 1, 3),
    (RING, 1, DOWN, 1, 0), (RING, 1, UP, 1, 4), (RING, 1, DOWN, 1, 1), (RING, 1, UP, 1, 5),
    (RING, 1, DOWN, 1, 2), (LAST, 0, 0), (LAST, 0, 3), (LAST, 0, 1), (LAST, 0, 4), (LAST, 0, 2),
    (LAST, 0, 5), (RING, 1, UP, 1, 0), (RING, 1, DOWN, 1, 3), (RING, 1, UP, 1, 1),
    (RING, 1, DOWN, 1, 4), (RING, 1, UP, 1, 2), (RING, 1, DOWN, 1, 5), (RING, 1, UP, 2, 3),
    (RING, 1, DOWN, 2, 0), (RING, 1, UP, 2, 4), (RING, 1, DOWN, 2, 1), (RING, 1, UP, 2, 5),
    (RING, 1, DOWN, 2, 2), (RING, 1, UP, 2, 0), (RING, 1, DOWN, 2, 3), (RING, 1, UP, 2, 1),
    (RING, 1, DOWN, 2, 4), (RING, 1, UP, 2, 2), (RING, 1, DOWN, 2, 5), (RING, 1, UP, 3, 3),
    (RING, 1, DOWN, 3, 0), (RING, 1, UP, 3, 4), (RING, 1, DOWN, 3, 1), (RING, 1, UP, 3, 5),
    (RING, 1, DOWN, 3, 2), (RING, 1, UP, 3, 0), (RING, 1, DOWN, 3, 3), (RING, 1, UP, 3, 1),
    (RING, 1, DOWN, 3, 4), (RING, 1, UP, 3, 2), (RING, 1, DOWN, 3, 5), (LAST, 1, 0), (LAST, 1, 3),
    (LAST, 1, 1), (LAST, 1, 4), (LAST, 1, 2), (LAST, 1, 5), (FINISH,),
)

def rope_rows(positions, head_dim):
    half = head_dim // 2
    inverse = ROPE_BASE ** (-np.arange(half, dtype=np.float64) * 2.0 / head_dim)
    angles = np.asarray(positions, np.float64)[:, None] * inverse[None, :]
    cosine, sine = np.cos(angles), np.sin(angles)
    return (
        np.concatenate([cosine, cosine], axis=1).astype(np.float32),
        np.concatenate([-sine, sine], axis=1).astype(np.float32),
    )


def unit_rms(values):
    mean_square = jnp.mean(values * values, axis=-1, keepdims=True)
    return values * lax.rsqrt(mean_square + EPSILON)


def rotate(values, cosine, signed_sine):
    half = values.shape[-1] // 2
    return values * cosine + pltpu.roll(values, half, axis=1) * signed_sine


def nt_dot(left, right):
    return lax.dot_general(left, right, (((1,), (1,)), ((), ())), preferred_element_type=F32)


def kernel(
    hid_in, ing_in, wq_in, wk_in, wv_in, qg_in, kg_in, wo_in, og_in, ck_in, cv_in, tables_in,
    table, length_ref, tool,
    out,
    hid, ing, og, qg, kg, wo, ck, tables,
    tok, wb, kvb, wob, wsrc, wst, osrc, ost, term, ru, rd, ysend, yrecv, total,
    proj, queries, seg_keys, seg_values, attended, att_acc, row_best, row_total,
    load_sems, send_sems, recv_sems,
):
    roll, head = lax.axis_index("roll"), lax.axis_index("head")
    x, yl, c = lax.div(roll, 8), lax.rem(lax.div(roll, 2), 4), lax.rem(roll, 2)
    z, yh = lax.div(head, 2), lax.rem(head, 2)
    own_rows, width = hid.shape
    slots, shard = table.shape[0], wq_in.shape[0]
    pair = 2 * shard
    block_rows = ck.shape[0]
    hd = qg.shape[1]
    own_cache = pl.ds(pl.multiple_of(roll * block_rows, 16), block_rows)

    loads = {}

    def load(name, src, dst):
        loads[name] = pltpu.make_async_copy(src, dst, load_sems.at[len(loads)])
        loads[name].start()

    def loaded(*names):
        for name in names:
            loads[name].wait()

    load("hid", hid_in, hid)
    load("ing", ing_in, ing)
    load("wq", wq_in, wsrc.at[0])
    load("wk", wk_in, wsrc.at[1, :, pl.ds(0, hd)])
    load("wv", wv_in, wsrc.at[1, :, pl.ds(hd, hd)])
    load("ck", ck_in, ck)
    load("cv", cv_in, kvb.at[own_cache, pl.ds(hd, hd)])
    load("tables", tables_in, tables)
    load("wo", wo_in, wo)
    load("qg", qg_in, qg)
    load("kg", kg_in, kg)
    load("og", og_in, og)
    seg = tok.shape[0]
    half_width = width // 2
    piece = width // PIECES

    def wrap(value, size):
        return lax.rem(value + size, size)

    def dev(x_=x, yl_=yl, c_=c, z_=z, yh_=yh):
        return {"roll": (x_ * NY + yl_) * NC + c_, "head": z_ * NH + yh_}

    sibling = dev(c_=1 - c)
    x_up, x_down = dev(x_=wrap(x + 1, NX)), dev(x_=wrap(x - 1, NX))
    z_up, z_down = dev(z_=wrap(z + 1, NZ)), dev(z_=wrap(z - 1, NZ))
    upper = lax.div(yl, 2)
    inner = yl + upper * (3 - 2 * yl)

    def mirrored(place):
        return place + upper * (3 - 2 * place)

    y_near = [yl, mirrored(1 - inner), mirrored(2), mirrored(3)]
    y_next = dev(yl_=y_near[1])
    y_end, y_middle = dev(yl_=mirrored(0)), dev(yl_=mirrored(2))
    partner = dev(yh_=1 - yh)

    index_of = {}
    started = []

    def slot_of(key):
        return index_of.setdefault(key, len(index_of))

    def copy_of(key, src, dst, where):
        i = slot_of(key)
        return pltpu.make_async_remote_copy(
            src_ref=src, dst_ref=dst, send_sem=send_sems.at[i], recv_sem=recv_sems.at[i],
            device_id=where, device_id_type=MESH,
        )

    def send(key, src, where, dst=None, when=None):
        copy = copy_of(key, src, src if dst is None else dst, where)
        if when is None:
            copy.start()
        else:
            pl.when(when)(copy.start)
        started.append((copy, when))

    def recv(key, dst):
        copy_of(key, dst, dst, sibling).wait_recv()

    barrier = pltpu.get_barrier_semaphore()
    for where in [sibling, x_up, x_down, z_up, z_down, partner, y_next]:
        pl.semaphore_signal(barrier, inc=1, device_id=where, device_id_type=MESH)

    @pl.when(inner == 1)
    def _():
        pl.semaphore_signal(barrier, inc=1, device_id=y_middle, device_id_type=MESH)

    loaded("hid", "ing")
    normed = unit_rms(hid[...].astype(F32)) * ing[...].reshape(1, width)
    tok[pl.ds(pl.multiple_of((yh * NZ + z) * own_rows, own_rows), own_rows), :] = normed.astype(BF16)
    loaded("wq", "wk", "wv")
    pl.semaphore_wait(barrier, 7 + inner)

    send("W sibling", wsrc.at[1 - c], sibling, wst)

    def token_block(zz, yy, part):
        return tok.at[
            pl.ds(pl.multiple_of((yy * NZ + zz) * own_rows, own_rows), own_rows),
            pl.ds(part * half_width, half_width),
        ]

    def token_key(group, way, distance, part):
        return ("T", group, way, distance, part)

    def token_own(group):
        yy = yh if group == 0 else 1 - yh
        for part in range(2):
            if group == 1:
                recv(("TP", part), token_block(z, yy, part))
            block = token_block(z, yy, part)
            send(token_key(group, UP, 1, part), block, z_up)
            send(token_key(group, DOWN, 1, part), block, z_down)

    def token_step(group, way, distance, part):
        yy = yh if group == 0 else 1 - yh
        sign, where, last = (-1, z_up, 0) if way == UP else (1, z_down, 1)
        block = token_block(wrap(z + sign * distance, NZ), yy, part)
        recv(token_key(group, way, distance, part), block)
        if distance < 3 or (distance == 3 and part == last):
            send(token_key(group, way, distance + 1, part), block, where)

    def token_partner():
        for part in range(2):
            send(("TP", part), token_block(z, yh, part), partner)

    token_own(0)

    class Gather:
        def __init__(self, name, rows):
            self.name, self.rows = name, rows
            self.steps = {
                OWN_Y: self.own_y, OWN_X: self.own_x, FROM_Y: self.y_step,
                FROM_X: self.x_step, FROM_OPPOSITE: self.o_step, ARRIVED: self.arrived,
            }

        def at(self, dx, i, k, core=c):
            return self.rows(wrap(x + dx, NX) * NY + y_near[i], core, k)

        def own_y(self, k):
            block = self.at(0, 0, k)
            send((self.name, "yn", k), block, y_next)
            send((self.name, "ym", 0, k), block, y_middle, when=inner == 1)

        def own_x(self, k):
            self.spread(0, k)

        def spread(self, i, k):
            block = self.at(0, i, k)
            send((self.name, UP, i, k), block, x_up)
            send((self.name, DOWN, i, k), block, x_down)
            send((self.name, "s", 0, i, k), block, sibling)

        def y_step(self, i, k):
            block = self.at(0, i, k)
            if i == 1:
                recv((self.name, "yn", k), block)
                send((self.name, "ym", 1, k), block, y_middle, when=inner == 1)
            else:
                @pl.when(inner == 1)
                def _():
                    recv((self.name, "ym", i - 2, k), block)

                @pl.when(inner == 0)
                def _():
                    recv((self.name, "ye", i, k), block)

                send((self.name, "ye", i, k), block, y_end, when=inner == 1)
            self.spread(i, k)

        def x_step(self, way, i, k):
            dx, where, last = (-1, x_up, 0) if way == UP else (1, x_down, 1)
            block = self.at(dx, i, k)
            recv((self.name, way, i, k), block)
            if k == last:
                send((self.name, "o", way, i), block, where)
            send((self.name, "s", dx, i, k), block, sibling)

        def o_step(self, way, i):
            k = 0 if way == UP else 1
            block = self.at(2, i, k)
            recv((self.name, "o", way, i), block)
            send((self.name, "s", 2, i, k), block, sibling)

        def arrived(self, dx):
            for i in range(NY):
                for k in range(2):
                    recv((self.name, "s", dx, i, k), self.at(dx, i, k, 1 - c))

    def pair_rows(ref):
        def rows(chip, core, k):
            start, size = pair_parts[k]
            return ref.at[core, pl.ds(pl.multiple_of(chip * pair + start, 16), size)]

        return rows

    def cache_rows(chip, core, k):
        start, size = cache_parts[k]
        return kvb.at[pl.ds(pl.multiple_of((chip * NC + core) * block_rows + start, 16), size)]

    pair_parts = ((0, 176), (176, 160))
    cache_parts = ((0, 80), (80, 80))
    gathers = {
        QKV: Gather("W", pair_rows(wb)),
        CACHE: Gather("C", cache_rows),
        OUT: Gather("O", pair_rows(wob)),
    }
    chip = x * NY + yl

    def join_pair(mine, other):
        mine, other = mine.astype(F32), other.astype(F32)
        upper = jnp.where(c == 0, mine, other)
        lower = jnp.where(c == 0, other, mine)
        return jnp.concatenate([upper, lower], axis=0).astype(BF16)

    recv("W sibling", wst)
    wb[c, pl.ds(pl.multiple_of(chip * pair, 16), pair), :] = join_pair(wsrc[c], wst[...])
    for k in range(2):
        gathers[QKV].own_y(k)
        gathers[QKV].own_x(k)
    token_partner()

    slot_block = table[roll]
    loaded("tables", "ck")
    first_seg = slots + block_rows
    block_cos, block_sin = tables[0:slots, 0:hd], tables[0:slots, hd : 2 * hd]
    row_cos, row_sin = tables[slots:first_seg, 0:hd], tables[slots:first_seg, hd : 2 * hd]
    seg_cos = tables[first_seg : first_seg + seg, 0:hd]
    seg_sin = tables[first_seg : first_seg + seg, hd : 2 * hd]
    pick = lax.broadcasted_iota(jnp.int32, (slots, hd), 0) == slot_block
    start_cos = jnp.sum(jnp.where(pick, block_cos, 0.0), axis=0, keepdims=True)
    start_sin = jnp.sum(jnp.where(pick, block_sin, 0.0), axis=0, keepdims=True)
    lane = lax.broadcasted_iota(jnp.int32, (1, hd), 1)
    sign = jnp.where(lane < hd // 2, -1.0, 1.0)
    cosine = start_cos * row_cos - start_sin * row_sin
    sine = (start_sin * row_cos + start_cos * row_sin) * sign
    kvb[own_cache, 0:hd] = rotate(ck[...].astype(F32), cosine, sine).astype(BF16)
    loaded("cv")

    loaded("wo", "qg", "kg")
    turned = wo[...]
    osrc[0] = turned[:, 0:hd]
    osrc[1] = turned[:, hd : 2 * hd]
    send("O sibling", osrc.at[1 - c], sibling, ost)

    rows = seg // NH

    def project_all():
        depth = 1792
        proj[...] = jnp.zeros_like(proj)

        def project(step, carry):
            at = pl.ds(pl.multiple_of(step * depth, depth), depth)
            tokens = tok[:, at]
            proj[:, 0 : 2 * hd] += jnp.dot(tokens, wb[0, at, :], preferred_element_type=F32)
            proj[:, 2 * hd : 4 * hd] += jnp.dot(tokens, wb[1, at, :], preferred_element_type=F32)
            return carry

        lax.fori_loop(0, width // depth, project, 0)
        for g in range(2):
            query = unit_rms(proj[:, g * hd : (g + 1) * hd]) * qg[...]
            query = rotate(query, seg_cos, seg_sin).astype(BF16)
            for yy in range(NH):
                queries[yy, g * rows : (g + 1) * rows, :] = query[yy * rows : (yy + 1) * rows]
        key = unit_rms(proj[:, 2 * hd : 3 * hd]) * kg[...]
        seg_keys[...] = rotate(key, seg_cos, seg_sin).astype(BF16)
        seg_values[...] = proj[:, 3 * hd : 4 * hd].astype(BF16)

    scale = 1.0 / QSCALE**0.5 / math.log(2.0)
    length = length_ref[0]
    group_y = (1 - yh, yh)

    def exponentials(scores, best):
        return [
            jnp.exp2((scores[:, j : j + hd] - best) * scale) for j in range(0, scores.shape[1], hd)
        ]

    def weighted(weights, values):
        weights = jnp.concatenate([part.astype(BF16) for part in weights], axis=1)
        return jnp.dot(weights, values, preferred_element_type=F32)

    def attend_segment(g):
        scores = nt_dot(queries[group_y[g]], seg_keys[...])
        row = lax.broadcasted_iota(jnp.int32, scores.shape, 0) & (rows - 1)
        row_t = row + (row >> 4) * 16 + group_y[g] * own_rows
        col = lax.broadcasted_iota(jnp.int32, scores.shape, 1)
        col_in = col & (rows - 1)
        col_t = col_in + (col_in >> 4) * 16 + (col >> 7) * own_rows
        scores = jnp.where((col_t <= row_t) & (col_t < length), scores, -1e30)
        best = jnp.broadcast_to(jnp.max(scores, axis=1, keepdims=True), row_best.shape)
        weights = exponentials(scores, best)
        row_best[...] = best
        row_total[...] = sum(weights[1:], weights[0])
        att_acc[...] = weighted(weights, seg_values[...])

    group_rows = NY * NC * block_rows

    def attend_group(g, dx):
        at = pl.ds(pl.multiple_of(wrap(x + dx, NX) * group_rows, 16), group_rows)
        scores = nt_dot(queries[group_y[g]], kvb[at, 0:hd])
        old_best = row_best[...]
        best = jnp.maximum(old_best, jnp.max(scores, axis=1, keepdims=True))
        rescale = jnp.exp2((old_best - best) * scale)
        weights = exponentials(scores, best)
        row_best[...] = best
        row_total[...] = row_total[...] * rescale + sum(weights[1:], weights[0])
        att_acc[...] = att_acc[...] * rescale + weighted(weights, kvb[at, hd : 2 * hd])

    def close_group(g):
        combined = att_acc[...] / jnp.sum(row_total[...], axis=1, keepdims=True)
        combined = combined.astype(BF16)
        for half in range(2):
            attended[g, :, half * hd : (half + 1) * hd] = combined[half * rows : (half + 1) * rows]

    def term_at(g, dz, p):
        return (
            pl.ds(
                pl.multiple_of((group_y[g] * NZ + wrap(z + dz, NZ)) * own_rows, own_rows), own_rows
            ),
            pl.ds(p * piece, piece),
        )

    def make_term(g, p):
        at = pl.ds(p * piece, piece)
        columns = jnp.concatenate([wob[0, at, :], wob[1, at, :]], axis=1)
        place = pl.ds(pl.multiple_of(group_y[g] * rows, rows), rows)
        term[place, at] = nt_dot(attended[g], columns).astype(BF16)

    def ring_step(g, way, k, p):
        sign, where, buf = (1, z_up, ru) if way == UP else (-1, z_down, rd)
        at = term_at(g, sign * (4 - k), p)
        first_piece = (p < PIECES // 2) == (way == UP)
        if k >= 2 or (k == 1 and first_piece):
            recv(("R", g, way, k - 1, p), buf.at[g, k - 1, p])
            term[at] = (term[at].astype(F32) + buf[g, k - 1, p].astype(F32)).astype(BF16)
        send(("R", g, way, k, p), term.at[at], where, buf.at[g, k, p])

    def ring_last(g, p):
        recv(("R", g, UP, 3, p), ru.at[g, 3, p])
        recv(("R", g, DOWN, 3, p), rd.at[g, 3, p])
        summed = (
            term[term_at(g, 0, p)].astype(F32)
            + ru[g, 3, p].astype(F32)
            + rd[g, 3, p].astype(F32)
        )
        if g == 0:
            ysend[p] = summed.astype(BF16)
            send(("Y", p), ysend.at[p], partner, yrecv.at[p])
        else:
            recv(("Y", p), yrecv.at[p])
            total[:, p * piece : (p + 1) * piece] = summed + yrecv[p].astype(F32)

    def finish():
        loaded("og")
        branch = unit_rms(total[...]) * og[...].reshape(1, width)
        row_i = lax.broadcasted_iota(jnp.int32, (own_rows, 1), 0)
        masked = jnp.zeros((own_rows, 1), jnp.int32)
        for t in range(own_rows):
            masked = jnp.where(row_i == t, tool[0, t], masked)
        keep = jnp.where((head * own_rows + row_i < length) & (masked == 0), 1.0, 0.0)
        out[...] = ((hid[...].astype(F32) + branch) * keep).astype(BF16)

    def own_out_ready():
        recv("O sibling", ost)
        wob[c, pl.ds(pl.multiple_of(chip * pair, 16), pair), :] = join_pair(osrc[c], ost[...])

    steps = {
        TOKENS: token_step, TOKENS_OWN: token_own, READY: own_out_ready, PROJECT: project_all,
        SEGMENT: attend_segment, ATTEND: attend_group, CLOSE: close_group,
        TERM: make_term, RING: ring_step, LAST: ring_last, FINISH: finish,
    }

    for op, *what in ORDER:
        if op in steps:
            steps[op](*what)
        else:
            gathers[what[0]].steps[op](*what[1:])

    for copy, when in started:
        if when is None:
            copy.wait_send()
        else:
            pl.when(when)(copy.wait_send)


def on_device(
    hidden, in_gain, w_query, w_key, w_value, q_gain, k_gain, w_out, out_gain,
    cache_keys, cache_values, block_table, seg_length, tool_mask,
):
    own_rows, width = hidden.shape[1:]
    hd = q_gain.shape[0]
    slots = block_table.shape[0]
    block_rows = cache_keys.shape[0]
    seg = own_rows * NZ * NH
    shard = w_query.shape[0]
    half = hd // 2
    block_cos, block_sin = rope_rows(np.arange(slots) * block_rows, hd)
    row_cos, row_sin = rope_rows(np.arange(block_rows), hd)
    block_sin = np.concatenate([block_sin[:, half:], block_sin[:, half:]], axis=1)
    row_sin = np.concatenate([row_sin[:, half:], row_sin[:, half:]], axis=1)
    tokens = np.arange(seg).reshape(NZ, NH, own_rows).transpose(1, 0, 2).reshape(-1)
    seg_cos, seg_sin = rope_rows(slots * block_rows + tokens, hd)
    tables = np.concatenate(
        [
            np.concatenate([block_cos, row_cos, seg_cos], axis=0),
            np.concatenate([block_sin, row_sin, seg_sin], axis=0),
        ],
        axis=1,
    )
    piece = width // PIECES
    vmem = pl.BlockSpec(memory_space=pltpu.VMEM)
    smem = pl.BlockSpec(memory_space=pltpu.SMEM)
    copies = 340
    result = pl.pallas_call(
        kernel,
        out_shape=jax.ShapeDtypeStruct((own_rows, width), BF16),
        in_specs=[pl.BlockSpec(memory_space=pl.ANY)] * 12 + [smem] * 3,
        out_specs=vmem,
        scratch_shapes=[
            pltpu.VMEM((own_rows, width), BF16),
            pltpu.VMEM((width,), F32),
            pltpu.VMEM((width,), F32),
            pltpu.VMEM((1, hd), F32),
            pltpu.VMEM((1, hd), F32),
            pltpu.VMEM((shard, 2 * hd), BF16),
            pltpu.VMEM((block_rows, hd), BF16),
            pltpu.VMEM(tables.shape, F32),
            pltpu.VMEM((seg, width), BF16),
            pltpu.VMEM((2, width, 2 * hd), BF16),
            pltpu.VMEM((slots * block_rows, 2 * hd), BF16),
            pltpu.VMEM((2, width, hd), BF16),
            pltpu.VMEM((2, shard, 2 * hd), BF16),
            pltpu.VMEM((shard, 2 * hd), BF16),
            pltpu.VMEM((2, shard, hd), BF16),
            pltpu.VMEM((shard, hd), BF16),
            pltpu.VMEM((seg, width), BF16),
            pltpu.VMEM((2, 4, PIECES, own_rows, piece), BF16),
            pltpu.VMEM((2, 4, PIECES, own_rows, piece), BF16),
            pltpu.VMEM((PIECES, own_rows, piece), BF16),
            pltpu.VMEM((PIECES, own_rows, piece), BF16),
            pltpu.VMEM((own_rows, width), F32),
            pltpu.VMEM((seg, 4 * hd), F32),
            pltpu.VMEM((NH, seg, hd), BF16),
            pltpu.VMEM((seg, hd), BF16),
            pltpu.VMEM((seg, hd), BF16),
            pltpu.VMEM((2, seg // NH, 2 * hd), BF16),
            pltpu.VMEM((seg, hd), F32),
            pltpu.VMEM((seg, hd), F32),
            pltpu.VMEM((seg, hd), F32),
            pltpu.SemaphoreType.DMA((12,)),
            pltpu.SemaphoreType.DMA((copies,)),
            pltpu.SemaphoreType.DMA((copies,)),
        ],
        compiler_params=pltpu.CompilerParams(
            collective_id=0, has_side_effects=True, vmem_limit_bytes=56 * 2**20
        ),
    )(
        hidden[0], in_gain, w_query, w_key, w_value, q_gain.reshape(1, -1), k_gain.reshape(1, -1),
        w_out.T, out_gain, cache_keys, cache_values, tables,
        block_table, seg_length, tool_mask,
    )
    return result[None]


def solution(mesh):
    return jax.shard_map(
        on_device,
        mesh=mesh,
        in_specs=(
            P("roll", "head", None),
            P(),
            P("roll", "head"),
            P("roll", "head"),
            P("roll", "head"),
            P(),
            P(),
            P("head", "roll"),
            P(),
            P("roll", "head"),
            P("roll", "head"),
            P(),
            P("roll"),
            P("roll", "head"),
        ),
        out_specs=P("roll", "head", None),
        check_vma=False,
    )
```

```python
import math

import jax
import jax.numpy as jnp
import numpy as np
from jax import lax
from jax.experimental import pallas as pl
from jax.experimental.pallas import tpu as pltpu
from jax.sharding import PartitionSpec as P

QSCALE = 168
EPSILON = 1e-06
ROPE_BASE = 1000000.0
MESH = pl.DeviceIdType.MESH
F32 = jnp.float32
BF16 = jnp.bfloat16

NX, NY, NC, NZ, NH = 4, 4, 2, 8, 2
PIECES = 6

(
    TOKENS, TOKENS_OWN, READY, PROJECT, SEGMENT, ATTEND, CLOSE, TERM, RING, SWAP, ADD, LAST, FINISH,
    OWN_Y, OWN_X, FROM_Y, FROM_X, FROM_OPPOSITE, ARRIVED,
    FIRST_OWN_X, FIRST_OWN_Y, FIRST_FROM_X, FIRST_FROM_OPPOSITE, FIRST_FROM_Y,
) = range(24)
UP, DOWN = range(2)
QKV, CACHE, OUT = range(3)
ORDER = (
    (OWN_Y, CACHE, 0), (TOKENS, 0, DOWN, 1, 0), (OWN_X, CACHE, 0), (TOKENS, 0, UP, 1, 0),
    (FROM_Y, QKV, 1, 0), (TOKENS, 0, UP, 1, 1), (FROM_Y, QKV, 1, 1), (FROM_X, QKV, DOWN, 0, 1),
    (READY,), (OWN_X, OUT, 0), (FROM_X, QKV, UP, 1, 0), (FROM_X, CACHE, DOWN, 0, 0),
    (FIRST_OWN_X, CACHE), (TOKENS, 0, UP, 2, 1), (FROM_X, QKV, DOWN, 1, 0), (OWN_X, OUT, 1),
    (TOKENS, 0, DOWN, 1, 1), (FROM_Y, CACHE, 1, 0), (FROM_X, CACHE, UP, 0, 0),
    (FROM_X, QKV, UP, 0, 0), (FIRST_OWN_Y, CACHE), (FROM_X, QKV, UP, 0, 1), (TOKENS, 0, DOWN, 2, 0),
    (FROM_Y, QKV, 2, 1), (FROM_X, QKV, DOWN, 1, 1), (TOKENS_OWN, 1), (FROM_Y, QKV, 2, 0),
    (TOKENS, 0, DOWN, 2, 1), (FROM_Y, QKV, 3, 0), (OWN_Y, OUT, 1), (TOKENS, 1, UP, 1, 0),
    (TOKENS, 0, UP, 2, 0), (FROM_Y, QKV, 3, 1), (TOKENS, 1, DOWN, 1, 1),
    (FIRST_FROM_Y, CACHE, 0, 1), (FROM_Y, CACHE, 3, 0), (FROM_X, QKV, DOWN, 2, 1),
    (TOKENS, 1, UP, 1, 1), (FROM_OPPOSITE, QKV, DOWN, 0), (OWN_Y, OUT, 0), (FROM_X, OUT, UP, 0, 1),
    (FIRST_FROM_X, CACHE, DOWN), (FIRST_FROM_X, CACHE, UP), (FROM_OPPOSITE, QKV, UP, 0),
    (TOKENS, 1, DOWN, 1, 0), (TOKENS, 0, DOWN, 3, 1), (FROM_X, QKV, UP, 2, 0),
    (TOKENS, 1, UP, 2, 0), (FROM_X, QKV, UP, 2, 1), (TOKENS, 1, DOWN, 2, 1), (FROM_Y, OUT, 1, 1),
    (FIRST_FROM_Y, CACHE, 0, 2), (FIRST_FROM_Y, CACHE, 0, 3), (FROM_X, QKV, DOWN, 0, 0),
    (TOKENS, 0, UP, 3, 0), (FROM_X, QKV, UP, 3, 0), (TOKENS, 1, DOWN, 2, 0),
    (FROM_X, QKV, DOWN, 3, 1), (FROM_OPPOSITE, QKV, UP, 1), (FROM_Y, CACHE, 2, 0),
    (FROM_X, QKV, UP, 1, 1), (TOKENS, 0, DOWN, 4, 1), (TOKENS, 1, UP, 2, 1), (FROM_Y, OUT, 2, 1),
    (FROM_Y, OUT, 2, 0), (ARRIVED, QKV, 0), (FROM_OPPOSITE, QKV, DOWN, 2), (TOKENS, 1, UP, 3, 0),
    (FROM_Y, OUT, 1, 0), (FROM_X, QKV, DOWN, 2, 0), (FROM_Y, OUT, 3, 1), (TOKENS, 1, DOWN, 3, 1),
    (FROM_X, QKV, UP, 3, 1), (FIRST_FROM_Y, CACHE, -1, 1), (TOKENS, 0, DOWN, 3, 0),
    (FROM_X, OUT, DOWN, 0, 0), (FROM_X, QKV, DOWN, 3, 0), (FIRST_FROM_Y, CACHE, 1, 1),
    (FIRST_FROM_OPPOSITE, CACHE), (FROM_X, OUT, DOWN, 0, 1), (FROM_X, OUT, UP, 1, 1),
    (FROM_OPPOSITE, QKV, UP, 3), (FROM_X, CACHE, UP, 1, 0), (FROM_X, OUT, DOWN, 1, 1),
    (FROM_OPPOSITE, QKV, DOWN, 1), (FROM_X, CACHE, DOWN, 1, 0), (TOKENS, 0, UP, 4, 0),
    (FROM_Y, OUT, 3, 0), (FROM_OPPOSITE, QKV, UP, 2), (FROM_X, OUT, UP, 0, 0),
    (FROM_X, CACHE, UP, 3, 0), (TOKENS, 1, UP, 3, 1), (FROM_OPPOSITE, QKV, DOWN, 3),
    (TOKENS, 0, UP, 3, 1), (TOKENS, 1, DOWN, 3, 0), (FIRST_FROM_Y, CACHE, -1, 2), (ARRIVED, QKV, 1),
    (FROM_X, CACHE, DOWN, 3, 0), (ARRIVED, QKV, -1), (ARRIVED, QKV, 2), (TOKENS, 1, UP, 4, 0),
    (TOKENS, 1, DOWN, 4, 1), (PROJECT,), (SEGMENT, 0), (FROM_X, OUT, UP, 1, 0),
    (FIRST_FROM_Y, CACHE, -1, 3), (FROM_X, CACHE, UP, 2, 0), (FIRST_FROM_Y, CACHE, 2, 1),
    (FROM_X, OUT, DOWN, 3, 1), (FIRST_FROM_Y, CACHE, 1, 2), (FROM_X, OUT, UP, 2, 0),
    (ARRIVED, CACHE, 0), (ATTEND, 0, 0), (FROM_X, OUT, UP, 3, 1), (FIRST_FROM_Y, CACHE, 1, 3),
    (FROM_X, OUT, DOWN, 2, 1), (FROM_X, CACHE, DOWN, 2, 0), (FROM_X, OUT, DOWN, 2, 0),
    (FROM_OPPOSITE, CACHE, UP, 1), (FROM_X, OUT, DOWN, 1, 0), (ARRIVED, CACHE, -1),
    (FROM_X, OUT, UP, 3, 0), (FROM_X, OUT, DOWN, 3, 0), (FIRST_FROM_Y, CACHE, 2, 2),
    (ATTEND, 0, -1), (FROM_OPPOSITE, CACHE, UP, 0), (FIRST_FROM_Y, CACHE, 2, 3),
    (FROM_OPPOSITE, CACHE, UP, 3), (ARRIVED, CACHE, 1), (FROM_OPPOSITE, CACHE, UP, 2),
    (ATTEND, 0, 1), (FROM_X, OUT, UP, 2, 1), (ARRIVED, CACHE, 2), (ATTEND, 0, 2), (ARRIVED, OUT, 0),
    (ARRIVED, OUT, -1), (ARRIVED, OUT, 1), (CLOSE, 0), (TERM, 0, 0), (SWAP,), (TERM, 0, 1),
    (RING, 0, UP, 0, 1), (RING, 0, DOWN, 1, 1), (TERM, 0, 2), (RING, 0, UP, 0, 2),
    (RING, 0, DOWN, 1, 2), (TERM, 0, 3), (RING, 0, DOWN, 0, 3), (RING, 0, UP, 1, 3),
    (FROM_OPPOSITE, OUT, DOWN, 0), (FROM_OPPOSITE, OUT, UP, 1), (FROM_OPPOSITE, OUT, UP, 0),
    (FROM_OPPOSITE, OUT, DOWN, 3), (FROM_OPPOSITE, OUT, DOWN, 1), (FROM_OPPOSITE, OUT, DOWN, 2),
    (FROM_OPPOSITE, OUT, UP, 2), (FROM_OPPOSITE, OUT, UP, 3), (ARRIVED, OUT, 2), (TERM, 0, 4),
    (RING, 0, DOWN, 0, 4), (RING, 0, UP, 1, 4), (TERM, 0, 5), (RING, 0, DOWN, 0, 5),
    (RING, 0, UP, 1, 5), (SEGMENT, 1), (ATTEND, 1, 0), (RING, 0, UP, 1, 1), (RING, 0, DOWN, 1, 3),
    (RING, 0, UP, 1, 2), (RING, 0, DOWN, 1, 4), (RING, 0, DOWN, 1, 5), (ATTEND, 1, -1),
    (ATTEND, 1, 1), (RING, 0, UP, 2, 3), (RING, 0, DOWN, 2, 1), (RING, 0, UP, 2, 4),
    (RING, 0, DOWN, 2, 2), (RING, 0, UP, 2, 5), (RING, 0, DOWN, 2, 3), (RING, 0, UP, 2, 1),
    (RING, 0, DOWN, 2, 4), (RING, 0, UP, 2, 2), (RING, 0, DOWN, 2, 5), (ATTEND, 1, 2), (CLOSE, 1),
    (RING, 0, UP, 3, 3), (RING, 0, DOWN, 3, 1), (RING, 0, UP, 3, 4), (RING, 0, DOWN, 3, 2),
    (RING, 0, UP, 3, 5), (RING, 0, DOWN, 3, 3), (RING, 0, UP, 3, 1), (RING, 0, DOWN, 3, 4),
    (RING, 0, UP, 3, 2), (RING, 0, DOWN, 3, 5), (TERM, 1, 1), (RING, 1, UP, 0, 1), (TERM, 1, 3),
    (RING, 1, DOWN, 0, 3), (TERM, 1, 2), (RING, 1, UP, 0, 2), (TERM, 1, 4), (RING, 1, DOWN, 0, 4),
    (TERM, 1, 5), (RING, 1, DOWN, 0, 5), (RING, 1, UP, 1, 3), (RING, 1, DOWN, 1, 1),
    (RING, 1, UP, 1, 4), (RING, 1, DOWN, 1, 2), (RING, 1, UP, 1, 5), (TERM, 1, 0), (ADD,),
    (RING, 1, UP, 0, 0), (RING, 1, DOWN, 1, 0), (RING, 1, UP, 1, 1), (RING, 1, DOWN, 1, 3),
    (RING, 1, UP, 1, 2), (RING, 1, DOWN, 1, 4), (RING, 1, DOWN, 1, 5), (LAST, 0, 1), (LAST, 0, 3),
    (LAST, 0, 2), (LAST, 0, 4), (LAST, 0, 5), (RING, 1, UP, 1, 0), (RING, 1, UP, 2, 3),
    (RING, 1, DOWN, 2, 1), (RING, 1, UP, 2, 4), (RING, 1, DOWN, 2, 2), (RING, 1, UP, 2, 5),
    (RING, 1, DOWN, 2, 0), (RING, 1, UP, 2, 1), (RING, 1, DOWN, 2, 3), (RING, 1, UP, 2, 2),
    (RING, 1, DOWN, 2, 4), (RING, 1, UP, 2, 0), (RING, 1, DOWN, 2, 5), (RING, 1, UP, 3, 3),
    (RING, 1, DOWN, 3, 1), (RING, 1, UP, 3, 4), (RING, 1, DOWN, 3, 2), (RING, 1, UP, 3, 5),
    (RING, 1, DOWN, 3, 0), (RING, 1, UP, 3, 1), (RING, 1, DOWN, 3, 3), (RING, 1, UP, 3, 2),
    (RING, 1, DOWN, 3, 4), (RING, 1, UP, 3, 0), (RING, 1, DOWN, 3, 5), (LAST, 1, 3), (LAST, 1, 1),
    (LAST, 1, 4), (LAST, 1, 2), (LAST, 1, 5), (LAST, 1, 0), (FINISH,),
)

def rope_rows(positions, head_dim):
    half = head_dim // 2
    inverse = ROPE_BASE ** (-np.arange(half, dtype=np.float64) * 2.0 / head_dim)
    angles = np.asarray(positions, np.float64)[:, None] * inverse[None, :]
    cosine, sine = np.cos(angles), np.sin(angles)
    return (
        np.concatenate([cosine, cosine], axis=1).astype(np.float32),
        np.concatenate([-sine, sine], axis=1).astype(np.float32),
    )


def unit_rms(values):
    mean_square = jnp.mean(values * values, axis=-1, keepdims=True)
    return values * lax.rsqrt(mean_square + EPSILON)


def rotate(values, cosine, signed_sine):
    half = values.shape[-1] // 2
    return values * cosine + pltpu.roll(values, half, axis=1) * signed_sine


def nt_dot(left, right):
    return lax.dot_general(left, right, (((1,), (1,)), ((), ())), preferred_element_type=F32)


def kernel(
    hid_in, ing_in, wq_in, wk_in, wv_in, qg_in, kg_in, wo_in, og_in, ck_in, cv_in, tables_in,
    table, length_ref, tool,
    out,
    hid, ing, og, qg, kg, wo, ck, tables,
    tok, wb, kvb, wob, wsrc, wst, osrc, ost, term, ru, rd, ysend, yrecv, zbuf, total,
    proj, queries, seg_keys, seg_values, attended, att_acc, row_best, row_total,
    load_sems, send_sems, recv_sems,
):
    roll, head = lax.axis_index("roll"), lax.axis_index("head")
    x, yl, c = lax.div(roll, 8), lax.rem(lax.div(roll, 2), 4), lax.rem(roll, 2)
    z, yh = lax.div(head, 2), lax.rem(head, 2)
    own_rows, width = hid.shape
    slots, shard = table.shape[0], wq_in.shape[0]
    pair = 2 * shard
    block_rows = ck.shape[0]
    hd = qg.shape[1]
    own_cache = pl.ds(pl.multiple_of(roll * block_rows, 16), block_rows)

    loads = {}

    def load(name, src, dst):
        loads[name] = pltpu.make_async_copy(src, dst, load_sems.at[len(loads)])
        loads[name].start()

    def loaded(*names):
        for name in names:
            loads[name].wait()

    load("hid", hid_in, hid)
    load("ing", ing_in, ing)
    load("wq", wq_in, wsrc.at[0])
    load("wk", wk_in, wsrc.at[1, :, pl.ds(0, hd)])
    load("wv", wv_in, wsrc.at[1, :, pl.ds(hd, hd)])
    load("ck", ck_in, ck)
    load("cv", cv_in, kvb.at[own_cache, pl.ds(hd, hd)])
    load("tables", tables_in, tables)
    load("wo", wo_in, wo)
    load("qg", qg_in, qg)
    load("kg", kg_in, kg)
    load("og", og_in, og)
    seg = tok.shape[0]
    half_width = width // 2
    piece = width // PIECES

    def wrap(value, size):
        return lax.rem(value + size, size)

    def dev(x_=x, yl_=yl, c_=c, z_=z, yh_=yh):
        return {"roll": (x_ * NY + yl_) * NC + c_, "head": z_ * NH + yh_}

    sibling = dev(c_=1 - c)
    x_up, x_down = dev(x_=wrap(x + 1, NX)), dev(x_=wrap(x - 1, NX))
    z_up, z_down = dev(z_=wrap(z + 1, NZ)), dev(z_=wrap(z - 1, NZ))
    upper = lax.div(yl, 2)
    inner = yl + upper * (3 - 2 * yl)

    def mirrored(place):
        return place + upper * (3 - 2 * place)

    y_near = [yl, mirrored(1 - inner), mirrored(2), mirrored(3)]
    y_next = dev(yl_=y_near[1])
    y_end, y_middle = dev(yl_=mirrored(0)), dev(yl_=mirrored(2))
    partner = dev(yh_=1 - yh)

    index_of = {}
    started = []

    def slot_of(key):
        return index_of.setdefault(key, len(index_of))

    def copy_of(key, src, dst, where):
        i = slot_of(key)
        return pltpu.make_async_remote_copy(
            src_ref=src, dst_ref=dst, send_sem=send_sems.at[i], recv_sem=recv_sems.at[i],
            device_id=where, device_id_type=MESH,
        )

    def send(key, src, where, dst=None, when=None):
        copy = copy_of(key, src, src if dst is None else dst, where)
        if when is None:
            copy.start()
        else:
            pl.when(when)(copy.start)
        started.append((copy, when))

    def recv(key, dst):
        copy_of(key, dst, dst, sibling).wait_recv()

    barrier = pltpu.get_barrier_semaphore()
    for where in [sibling, x_up, x_down, z_up, z_down, partner, y_next]:
        pl.semaphore_signal(barrier, inc=1, device_id=where, device_id_type=MESH)

    @pl.when(inner == 1)
    def _():
        pl.semaphore_signal(barrier, inc=1, device_id=y_middle, device_id_type=MESH)

    loaded("hid", "ing")
    normed = unit_rms(hid[...].astype(F32)) * ing[...].reshape(1, width)
    tok[pl.ds(pl.multiple_of((yh * NZ + z) * own_rows, own_rows), own_rows), :] = normed.astype(BF16)
    loaded("wq", "wk", "wv")
    pl.semaphore_wait(barrier, 7 + inner)

    send("W sibling", wsrc.at[1 - c], sibling, wst)

    def token_block(zz, yy, part):
        return tok.at[
            pl.ds(pl.multiple_of((yy * NZ + zz) * own_rows, own_rows), own_rows),
            pl.ds(part * half_width, half_width),
        ]

    def token_key(group, way, distance, part):
        return ("T", group, way, distance, part)

    def token_own(group):
        yy = yh if group == 0 else 1 - yh
        for part in range(2):
            if group == 1:
                recv(("TP", part), token_block(z, yy, part))
            block = token_block(z, yy, part)
            send(token_key(group, UP, 1, part), block, z_up)
            send(token_key(group, DOWN, 1, part), block, z_down)

    def token_step(group, way, distance, part):
        yy = yh if group == 0 else 1 - yh
        sign, where, last = (-1, z_up, 0) if way == UP else (1, z_down, 1)
        block = token_block(wrap(z + sign * distance, NZ), yy, part)
        recv(token_key(group, way, distance, part), block)
        if distance < 3 or (distance == 3 and part == last):
            send(token_key(group, way, distance + 1, part), block, where)

    def token_partner():
        for part in range(2):
            send(("TP", part), token_block(z, yh, part), partner)

    token_own(0)

    class Gather:
        def __init__(self, name, rows):
            self.name, self.rows = name, rows
            self.steps = {
                OWN_Y: self.own_y, OWN_X: self.own_x, FROM_Y: self.y_step,
                FROM_X: self.x_step, FROM_OPPOSITE: self.o_step, ARRIVED: self.arrived,
                FIRST_OWN_X: self.first_own_x, FIRST_OWN_Y: self.first_own_y,
                FIRST_FROM_X: self.first_from_x, FIRST_FROM_OPPOSITE: self.first_from_opposite,
                FIRST_FROM_Y: self.first_from_y,
            }

        def at(self, dx, i, k, core=c):
            return self.rows(wrap(x + dx, NX) * NY + y_near[i], core, k)

        def own_y(self, k):
            block = self.at(0, 0, k)
            send((self.name, "yn", k), block, y_next)
            send((self.name, "ym", 0, k), block, y_middle, when=inner == 1)

        def own_x(self, k):
            self.spread(0, k)

        def spread(self, i, k):
            block = self.at(0, i, k)
            send((self.name, UP, i, k), block, x_up)
            send((self.name, DOWN, i, k), block, x_down)
            send((self.name, "s", 0, i, k), block, sibling)

        def y_step(self, i, k):
            block = self.at(0, i, k)
            if i == 1:
                recv((self.name, "yn", k), block)
                send((self.name, "ym", 1, k), block, y_middle, when=inner == 1)
            else:
                @pl.when(inner == 1)
                def _():
                    recv((self.name, "ym", i - 2, k), block)

                @pl.when(inner == 0)
                def _():
                    recv((self.name, "ye", i, k), block)

                send((self.name, "ye", i, k), block, y_end, when=inner == 1)
            self.spread(i, k)

        def x_step(self, way, i, k):
            dx, where, last = (-1, x_up, 0) if way == UP else (1, x_down, 1)
            block = self.at(dx, i, k)
            recv((self.name, way, i, k), block)
            if k == last:
                send((self.name, "o", way, i), block, where)
            send((self.name, "s", dx, i, k), block, sibling)

        def o_step(self, way, i):
            k = 0 if way == UP else 1
            block = self.at(2, i, k)
            recv((self.name, "o", way, i), block)
            send((self.name, "s", 2, i, k), block, sibling)


        def first_y(self, dx):
            block = self.at(dx, 0, 1)
            send((self.name, "fyn", dx), block, y_next)
            send((self.name, "fym", dx, 0), block, y_middle, when=inner == 1)

        def first_own_x(self):
            block = self.at(0, 0, 1)
            send((self.name, "f", UP), block, x_up)
            send((self.name, "f", DOWN), block, x_down)
            send((self.name, "s", 0, 0, 1), block, sibling)

        def first_own_y(self):
            self.first_y(0)

        def first_from_x(self, way):
            dx, where = (-1, x_up) if way == UP else (1, x_down)
            block = self.at(dx, 0, 1)
            recv((self.name, "f", way), block)
            send((self.name, "fo", way), self.at(dx, 0, 2 + way), where)
            self.first_y(dx)
            send((self.name, "s", dx, 0, 1), block, sibling)

        def first_from_opposite(self):
            recv((self.name, "fo", UP), self.at(2, 0, 2 + UP))
            recv((self.name, "fo", DOWN), self.at(2, 0, 2 + DOWN))
            self.first_y(2)
            send((self.name, "s", 2, 0, 1), self.at(2, 0, 1), sibling)

        def first_from_y(self, dx, i):
            block = self.at(dx, i, 1)
            if i == 1:
                recv((self.name, "fyn", dx), block)
                send((self.name, "fym", dx, 1), block, y_middle, when=inner == 1)
            else:
                @pl.when(inner == 1)
                def _():
                    recv((self.name, "fym", dx, i - 2), block)

                @pl.when(inner == 0)
                def _():
                    recv((self.name, "fye", dx, i), block)

                send((self.name, "fye", dx, i), block, y_end, when=inner == 1)
            send((self.name, "s", dx, i, 1), block, sibling)

        def arrived(self, dx):
            for i in range(NY):
                for k in range(2):
                    recv((self.name, "s", dx, i, k), self.at(dx, i, k, 1 - c))

    def pair_rows(ref):
        def rows(chip, core, k):
            start, size = pair_parts[k]
            return ref.at[core, pl.ds(pl.multiple_of(chip * pair + start, 16), size)]

        return rows

    def cache_rows(chip, core, k):
        start, size = cache_parts[k]
        return kvb.at[pl.ds(pl.multiple_of((chip * NC + core) * block_rows + start, 16), size)]

    pair_parts = ((0, 176), (176, 160), (176, 80), (256, 80))
    cache_parts = ((0, 80), (80, 80), (80, 48), (128, 32))
    gathers = {
        QKV: Gather("W", pair_rows(wb)),
        CACHE: Gather("C", cache_rows),
        OUT: Gather("O", pair_rows(wob)),
    }
    chip = x * NY + yl

    def join_pair(mine, other):
        mine, other = mine.astype(F32), other.astype(F32)
        upper = jnp.where(c == 0, mine, other)
        lower = jnp.where(c == 0, other, mine)
        return jnp.concatenate([upper, lower], axis=0).astype(BF16)

    recv("W sibling", wst)
    wb[c, pl.ds(pl.multiple_of(chip * pair, 16), pair), :] = join_pair(wsrc[c], wst[...])
    for k in range(2):
        gathers[QKV].own_y(k)
        gathers[QKV].own_x(k)
    token_partner()

    slot_block = table[roll]
    loaded("tables", "ck")
    first_seg = slots + block_rows
    block_cos, block_sin = tables[0:slots, 0:hd], tables[0:slots, hd : 2 * hd]
    row_cos, row_sin = tables[slots:first_seg, 0:hd], tables[slots:first_seg, hd : 2 * hd]
    seg_cos = tables[first_seg : first_seg + seg, 0:hd]
    seg_sin = tables[first_seg : first_seg + seg, hd : 2 * hd]
    pick = lax.broadcasted_iota(jnp.int32, (slots, hd), 0) == slot_block
    start_cos = jnp.sum(jnp.where(pick, block_cos, 0.0), axis=0, keepdims=True)
    start_sin = jnp.sum(jnp.where(pick, block_sin, 0.0), axis=0, keepdims=True)
    lane = lax.broadcasted_iota(jnp.int32, (1, hd), 1)
    sign = jnp.where(lane < hd // 2, -1.0, 1.0)
    cosine = start_cos * row_cos - start_sin * row_sin
    sine = (start_sin * row_cos + start_cos * row_sin) * sign
    kvb[own_cache, 0:hd] = rotate(ck[...].astype(F32), cosine, sine).astype(BF16)
    loaded("cv")

    loaded("wo", "qg", "kg")
    turned = wo[...]
    osrc[0] = turned[:, 0:hd]
    osrc[1] = turned[:, hd : 2 * hd]
    send("O sibling", osrc.at[1 - c], sibling, ost)

    rows = seg // NH

    def project_all():
        depth = 1792
        proj[...] = jnp.zeros_like(proj)

        def project(step, carry):
            at = pl.ds(pl.multiple_of(step * depth, depth), depth)
            tokens = tok[:, at]
            proj[:, 0 : 2 * hd] += jnp.dot(tokens, wb[0, at, :], preferred_element_type=F32)
            proj[:, 2 * hd : 4 * hd] += jnp.dot(tokens, wb[1, at, :], preferred_element_type=F32)
            return carry

        lax.fori_loop(0, width // depth, project, 0)
        for g in range(2):
            query = unit_rms(proj[:, g * hd : (g + 1) * hd]) * qg[...]
            query = rotate(query, seg_cos, seg_sin).astype(BF16)
            for yy in range(NH):
                queries[yy, g * rows : (g + 1) * rows, :] = query[yy * rows : (yy + 1) * rows]
        key = unit_rms(proj[:, 2 * hd : 3 * hd]) * kg[...]
        seg_keys[...] = rotate(key, seg_cos, seg_sin).astype(BF16)
        seg_values[...] = proj[:, 3 * hd : 4 * hd].astype(BF16)

    scale = 1.0 / QSCALE**0.5 / math.log(2.0)
    length = length_ref[0]
    group_y = (1 - yh, yh)

    def exponentials(scores, best):
        return [
            jnp.exp2((scores[:, j : j + hd] - best) * scale) for j in range(0, scores.shape[1], hd)
        ]

    def weighted(weights, values):
        weights = jnp.concatenate([part.astype(BF16) for part in weights], axis=1)
        return jnp.dot(weights, values, preferred_element_type=F32)

    def attend_segment(g):
        scores = nt_dot(queries[group_y[g]], seg_keys[...])
        row = lax.broadcasted_iota(jnp.int32, scores.shape, 0) & (rows - 1)
        row_t = row + (row >> 4) * 16 + group_y[g] * own_rows
        col = lax.broadcasted_iota(jnp.int32, scores.shape, 1)
        col_in = col & (rows - 1)
        col_t = col_in + (col_in >> 4) * 16 + (col >> 7) * own_rows
        scores = jnp.where((col_t <= row_t) & (col_t < length), scores, -1e30)
        best = jnp.broadcast_to(jnp.max(scores, axis=1, keepdims=True), row_best.shape)
        weights = exponentials(scores, best)
        row_best[...] = best
        row_total[...] = sum(weights[1:], weights[0])
        att_acc[...] = weighted(weights, seg_values[...])

    group_rows = NY * NC * block_rows

    def attend_group(g, dx):
        at = pl.ds(pl.multiple_of(wrap(x + dx, NX) * group_rows, 16), group_rows)
        scores = nt_dot(queries[group_y[g]], kvb[at, 0:hd])
        old_best = row_best[...]
        best = jnp.maximum(old_best, jnp.max(scores, axis=1, keepdims=True))
        rescale = jnp.exp2((old_best - best) * scale)
        weights = exponentials(scores, best)
        row_best[...] = best
        row_total[...] = row_total[...] * rescale + sum(weights[1:], weights[0])
        att_acc[...] = att_acc[...] * rescale + weighted(weights, kvb[at, hd : 2 * hd])

    def close_group(g):
        combined = att_acc[...] / jnp.sum(row_total[...], axis=1, keepdims=True)
        combined = combined.astype(BF16)
        for half in range(2):
            attended[g, :, half * hd : (half + 1) * hd] = combined[half * rows : (half + 1) * rows]

    x_half, x_odd = lax.div(x, 2), lax.rem(x, 2)

    def columns_of(p):
        near = x_half if p < 3 else 1 - x_half
        place = p + x_odd * (2 - 2 * p) if p < 3 else (5 - p) + x_odd * (2 * p - 8)
        return pl.ds(pl.multiple_of((near * 3 + place) * piece, 128), piece)

    def term_at(g, dz, p):
        return (
            pl.ds(
                pl.multiple_of((group_y[g] * NZ + wrap(z + dz, NZ)) * own_rows, own_rows), own_rows
            ),
            columns_of(p),
        )

    def make_term(g, p):
        at = columns_of(p)
        columns = jnp.concatenate([wob[0, at, :], wob[1, at, :]], axis=1)
        place = pl.ds(pl.multiple_of(group_y[g] * rows, rows), rows)
        term[place, at] = nt_dot(attended[g], columns).astype(BF16)

    def ring_step(g, way, k, p):
        sign, where, buf = (1, z_up, ru) if way == UP else (-1, z_down, rd)
        at = term_at(g, sign * (4 - k), p)
        first_piece = (p < PIECES // 2) == (way == UP)
        if k >= 2 or (k == 1 and first_piece):
            recv(("R", g, way, k - 1, p), buf.at[g, k - 1, p])
            term[at] = (term[at].astype(F32) + buf[g, k - 1, p].astype(F32)).astype(BF16)
        send(("R", g, way, k, p), term.at[at], where, buf.at[g, k, p])

    def swap_terms():
        place = pl.ds(pl.multiple_of(group_y[0] * rows, rows), rows)
        send(("Z",), term.at[place, columns_of(0)], partner, zbuf)

    def add_swapped():
        recv(("Z",), zbuf)
        at = (pl.ds(pl.multiple_of(group_y[1] * rows, rows), rows), columns_of(0))
        term[at] = (term[at].astype(F32) + zbuf[...].astype(F32)).astype(BF16)

    def ring_last(g, p):
        recv(("R", g, UP, 3, p), ru.at[g, 3, p])
        recv(("R", g, DOWN, 3, p), rd.at[g, 3, p])
        summed = (
            term[term_at(g, 0, p)].astype(F32)
            + ru[g, 3, p].astype(F32)
            + rd[g, 3, p].astype(F32)
        )
        if g == 0:
            ysend[p] = summed.astype(BF16)
            send(("Y", p), ysend.at[p], partner, yrecv.at[p])
        elif p == 0:
            total[:, columns_of(p)] = summed
        else:
            recv(("Y", p), yrecv.at[p])
            total[:, columns_of(p)] = summed + yrecv[p].astype(F32)

    def finish():
        loaded("og")
        branch = unit_rms(total[...]) * og[...].reshape(1, width)
        row_i = lax.broadcasted_iota(jnp.int32, (own_rows, 1), 0)
        masked = jnp.zeros((own_rows, 1), jnp.int32)
        for t in range(own_rows):
            masked = jnp.where(row_i == t, tool[0, t], masked)
        keep = jnp.where((head * own_rows + row_i < length) & (masked == 0), 1.0, 0.0)
        out[...] = ((hid[...].astype(F32) + branch) * keep).astype(BF16)

    def own_out_ready():
        recv("O sibling", ost)
        wob[c, pl.ds(pl.multiple_of(chip * pair, 16), pair), :] = join_pair(osrc[c], ost[...])

    steps = {
        TOKENS: token_step, TOKENS_OWN: token_own, READY: own_out_ready, PROJECT: project_all,
        SEGMENT: attend_segment, ATTEND: attend_group, CLOSE: close_group,
        TERM: make_term, RING: ring_step, SWAP: swap_terms, ADD: add_swapped, LAST: ring_last, FINISH: finish,
    }

    for op, *what in ORDER:
        if op in steps:
            steps[op](*what)
        else:
            gathers[what[0]].steps[op](*what[1:])

    for copy, when in started:
        if when is None:
            copy.wait_send()
        else:
            pl.when(when)(copy.wait_send)


def on_device(
    hidden, in_gain, w_query, w_key, w_value, q_gain, k_gain, w_out, out_gain,
    cache_keys, cache_values, block_table, seg_length, tool_mask,
):
    own_rows, width = hidden.shape[1:]
    hd = q_gain.shape[0]
    slots = block_table.shape[0]
    block_rows = cache_keys.shape[0]
    seg = own_rows * NZ * NH
    shard = w_query.shape[0]
    half = hd // 2
    block_cos, block_sin = rope_rows(np.arange(slots) * block_rows, hd)
    row_cos, row_sin = rope_rows(np.arange(block_rows), hd)
    block_sin = np.concatenate([block_sin[:, half:], block_sin[:, half:]], axis=1)
    row_sin = np.concatenate([row_sin[:, half:], row_sin[:, half:]], axis=1)
    tokens = np.arange(seg).reshape(NZ, NH, own_rows).transpose(1, 0, 2).reshape(-1)
    seg_cos, seg_sin = rope_rows(slots * block_rows + tokens, hd)
    tables = np.concatenate(
        [
            np.concatenate([block_cos, row_cos, seg_cos], axis=0),
            np.concatenate([block_sin, row_sin, seg_sin], axis=0),
        ],
        axis=1,
    )
    piece = width // PIECES
    vmem = pl.BlockSpec(memory_space=pltpu.VMEM)
    smem = pl.BlockSpec(memory_space=pltpu.SMEM)
    copies = 340
    result = pl.pallas_call(
        kernel,
        out_shape=jax.ShapeDtypeStruct((own_rows, width), BF16),
        in_specs=[pl.BlockSpec(memory_space=pl.ANY)] * 12 + [smem] * 3,
        out_specs=vmem,
        scratch_shapes=[
            pltpu.VMEM((own_rows, width), BF16),
            pltpu.VMEM((width,), F32),
            pltpu.VMEM((width,), F32),
            pltpu.VMEM((1, hd), F32),
            pltpu.VMEM((1, hd), F32),
            pltpu.VMEM((shard, 2 * hd), BF16),
            pltpu.VMEM((block_rows, hd), BF16),
            pltpu.VMEM(tables.shape, F32),
            pltpu.VMEM((seg, width), BF16),
            pltpu.VMEM((2, width, 2 * hd), BF16),
            pltpu.VMEM((slots * block_rows, 2 * hd), BF16),
            pltpu.VMEM((2, width, hd), BF16),
            pltpu.VMEM((2, shard, 2 * hd), BF16),
            pltpu.VMEM((shard, 2 * hd), BF16),
            pltpu.VMEM((2, shard, hd), BF16),
            pltpu.VMEM((shard, hd), BF16),
            pltpu.VMEM((seg, width), BF16),
            pltpu.VMEM((2, 4, PIECES, own_rows, piece), BF16),
            pltpu.VMEM((2, 4, PIECES, own_rows, piece), BF16),
            pltpu.VMEM((PIECES, own_rows, piece), BF16),
            pltpu.VMEM((PIECES, own_rows, piece), BF16),
            pltpu.VMEM((seg // NH, piece), BF16),
            pltpu.VMEM((own_rows, width), F32),
            pltpu.VMEM((seg, 4 * hd), F32),
            pltpu.VMEM((NH, seg, hd), BF16),
            pltpu.VMEM((seg, hd), BF16),
            pltpu.VMEM((seg, hd), BF16),
            pltpu.VMEM((2, seg // NH, 2 * hd), BF16),
            pltpu.VMEM((seg, hd), F32),
            pltpu.VMEM((seg, hd), F32),
            pltpu.VMEM((seg, hd), F32),
            pltpu.SemaphoreType.DMA((12,)),
            pltpu.SemaphoreType.DMA((copies,)),
            pltpu.SemaphoreType.DMA((copies,)),
        ],
        compiler_params=pltpu.CompilerParams(
            collective_id=0, has_side_effects=True, vmem_limit_bytes=56 * 2**20
        ),
    )(
        hidden[0], in_gain, w_query, w_key, w_value, q_gain.reshape(1, -1), k_gain.reshape(1, -1),
        w_out.T, out_gain, cache_keys, cache_values, tables,
        block_table, seg_length, tool_mask,
    )
    return result[None]


def solution(mesh):
    return jax.shard_map(
        on_device,
        mesh=mesh,
        in_specs=(
            P("roll", "head", None),
            P(),
            P("roll", "head"),
            P("roll", "head"),
            P("roll", "head"),
            P(),
            P(),
            P("head", "roll"),
            P(),
            P("roll", "head"),
            P("roll", "head"),
            P(),
            P("roll"),
            P("roll", "head"),
        ),
        out_specs=P("roll", "head", None),
        check_vma=False,
    )
```

```python
import math

import jax
import jax.numpy as jnp
import numpy as np
from jax import lax
from jax.experimental import pallas as pl
from jax.experimental.pallas import tpu as pltpu
from jax.sharding import PartitionSpec as P

QSCALE = 168
EPSILON = 1e-06
ROPE_BASE = 1000000.0
MESH = pl.DeviceIdType.MESH
F32 = jnp.float32
BF16 = jnp.bfloat16

NX, NY, NC, NZ, NH = 4, 4, 2, 8, 2
PIECES = 6

(
    TOKENS, TOKENS_SWAP, TOKENS_OWN, READY, PROJECT, SEGMENT, ATTEND, CLOSE, TERM, RING, SWAP, ADD, LAST, FINISH,
    OWN_Y, OWN_X, FROM_Y, FROM_X, FROM_OPPOSITE, ARRIVED,
    FIRST_OWN_X, FIRST_OWN_Y, FIRST_FROM_X, FIRST_FROM_OPPOSITE, FIRST_FROM_Y,
) = range(25)
UP, DOWN = range(2)
QKV, CACHE, OUT = range(3)
ORDER = (
    (READY,), (OWN_X, OUT, 0), (OWN_Y, CACHE, 0), (TOKENS, 0, UP, 1, 0), (TOKENS_SWAP, 0),
    (TOKENS, 0, DOWN, 1, 1), (OWN_X, CACHE, 0), (TOKENS_SWAP, 1), (FROM_Y, QKV, 1, 0),
    (OWN_X, OUT, 1), (TOKENS, 0, UP, 1, 1), (TOKENS, 0, DOWN, 1, 0), (FROM_X, CACHE, UP, 0, 0),
    (FROM_X, OUT, DOWN, 0, 0), (FROM_X, QKV, UP, 0, 0), (FIRST_OWN_X, CACHE), (FROM_Y, QKV, 1, 1),
    (FROM_Y, CACHE, 1, 0), (TOKENS, 0, DOWN, 2, 1), (TOKENS, 0, DOWN, 2, 0),
    (FROM_X, QKV, UP, 1, 0), (TOKENS_OWN, 0), (FIRST_OWN_Y, CACHE), (TOKENS, 0, UP, 2, 0),
    (FROM_X, QKV, DOWN, 0, 1), (FROM_Y, QKV, 2, 0), (TOKENS_OWN, 1), (FROM_Y, QKV, 2, 1),
    (FIRST_FROM_Y, CACHE, 0, 1), (OWN_Y, OUT, 1), (FROM_X, CACHE, DOWN, 0, 0),
    (FROM_X, QKV, DOWN, 1, 1), (TOKENS, 0, DOWN, 3, 1), (TOKENS, 1, UP, 1, 0),
    (FROM_X, OUT, UP, 0, 1), (FROM_Y, QKV, 3, 0), (TOKENS, 0, UP, 2, 1), (TOKENS, 1, DOWN, 1, 0),
    (FROM_Y, QKV, 3, 1), (OWN_Y, OUT, 0), (TOKENS, 1, DOWN, 1, 1), (TOKENS, 1, UP, 1, 1),
    (FROM_Y, CACHE, 3, 0), (FROM_X, QKV, UP, 0, 1), (FROM_OPPOSITE, QKV, DOWN, 0),
    (TOKENS, 1, UP, 2, 0), (FROM_X, QKV, DOWN, 1, 0), (FIRST_FROM_X, CACHE, UP),
    (FROM_X, QKV, UP, 2, 0), (FIRST_FROM_X, CACHE, DOWN), (FROM_X, QKV, UP, 2, 1),
    (FROM_X, QKV, DOWN, 2, 1), (TOKENS, 0, UP, 3, 0), (FROM_OPPOSITE, QKV, DOWN, 1),
    (FROM_Y, OUT, 1, 1), (FROM_X, QKV, DOWN, 3, 0), (FROM_X, QKV, DOWN, 2, 0),
    (TOKENS, 1, DOWN, 2, 1), (FROM_OPPOSITE, CACHE, UP, 0), (FROM_OPPOSITE, QKV, UP, 1),
    (FIRST_FROM_Y, CACHE, 0, 3), (TOKENS, 1, DOWN, 2, 0), (FROM_X, QKV, UP, 3, 0),
    (FROM_X, QKV, DOWN, 0, 0), (TOKENS, 0, DOWN, 4, 1), (FROM_Y, CACHE, 2, 0),
    (FROM_X, QKV, DOWN, 3, 1), (FROM_X, QKV, UP, 1, 1), (TOKENS, 1, UP, 2, 1), (ARRIVED, QKV, 0),
    (FROM_Y, OUT, 2, 1), (FROM_OPPOSITE, QKV, UP, 0), (FROM_Y, OUT, 1, 0),
    (FIRST_FROM_OPPOSITE, CACHE), (TOKENS, 1, UP, 3, 0), (FROM_Y, OUT, 3, 1),
    (TOKENS, 1, DOWN, 3, 1), (FROM_X, CACHE, UP, 3, 0), (FROM_OPPOSITE, QKV, DOWN, 2),
    (ARRIVED, QKV, 1), (FROM_X, QKV, UP, 3, 1), (FROM_Y, OUT, 2, 0), (FROM_Y, OUT, 3, 0),
    (TOKENS, 1, UP, 3, 1), (FIRST_FROM_Y, CACHE, 0, 2), (FROM_OPPOSITE, QKV, UP, 2),
    (FIRST_FROM_Y, CACHE, -1, 1), (FROM_X, CACHE, DOWN, 1, 0), (FROM_X, OUT, DOWN, 0, 1),
    (ARRIVED, QKV, -1), (FIRST_FROM_Y, CACHE, -1, 2), (FROM_X, CACHE, DOWN, 3, 0),
    (FROM_X, OUT, DOWN, 1, 1), (FROM_X, CACHE, UP, 1, 0), (TOKENS, 0, DOWN, 3, 0),
    (TOKENS, 1, UP, 4, 0), (FROM_X, CACHE, DOWN, 2, 0), (TOKENS, 0, UP, 3, 1),
    (FROM_OPPOSITE, QKV, DOWN, 3), (FIRST_FROM_Y, CACHE, 1, 1), (FROM_OPPOSITE, QKV, UP, 3),
    (TOKENS, 1, DOWN, 4, 1), (FIRST_FROM_Y, CACHE, 2, 2), (TOKENS, 1, DOWN, 3, 0),
    (ARRIVED, OUT, 0), (FROM_X, OUT, UP, 1, 1), (TOKENS, 0, UP, 4, 0), (FROM_X, CACHE, UP, 2, 0),
    (FROM_X, OUT, UP, 0, 0), (FROM_X, OUT, DOWN, 2, 1), (FIRST_FROM_Y, CACHE, 2, 1),
    (ARRIVED, QKV, 2), (FIRST_FROM_Y, CACHE, -1, 3), (PROJECT,), (SEGMENT, 0),
    (FIRST_FROM_Y, CACHE, 1, 3), (ARRIVED, CACHE, 0), (ATTEND, 0, 0), (FROM_X, OUT, DOWN, 3, 0),
    (FROM_X, OUT, UP, 1, 0), (FROM_X, OUT, DOWN, 2, 0), (FIRST_FROM_Y, CACHE, 1, 2),
    (FROM_X, OUT, DOWN, 3, 1), (FROM_X, OUT, DOWN, 1, 0), (ARRIVED, CACHE, -1),
    (FROM_X, OUT, UP, 3, 1), (FROM_X, OUT, UP, 2, 0), (ATTEND, 0, -1), (FIRST_FROM_Y, CACHE, 2, 3),
    (FROM_OPPOSITE, CACHE, UP, 1), (FROM_X, OUT, UP, 2, 1), (FROM_OPPOSITE, CACHE, UP, 3),
    (FROM_X, OUT, UP, 3, 0), (FROM_OPPOSITE, CACHE, UP, 2), (ARRIVED, CACHE, 1), (ARRIVED, OUT, 1),
    (ATTEND, 0, 1), (ARRIVED, OUT, -1), (ARRIVED, CACHE, 2), (ATTEND, 0, 2), (CLOSE, 0),
    (TERM, 0, 0), (SWAP,), (TERM, 0, 1), (RING, 0, UP, 0, 1), (RING, 0, DOWN, 1, 1), (TERM, 0, 2),
    (RING, 0, UP, 0, 2), (RING, 0, DOWN, 1, 2), (TERM, 0, 3), (RING, 0, DOWN, 0, 3),
    (RING, 0, UP, 1, 3), (FROM_OPPOSITE, OUT, UP, 1), (FROM_OPPOSITE, OUT, DOWN, 0),
    (FROM_OPPOSITE, OUT, DOWN, 1), (FROM_OPPOSITE, OUT, UP, 2), (FROM_OPPOSITE, OUT, UP, 3),
    (FROM_OPPOSITE, OUT, UP, 0), (FROM_OPPOSITE, OUT, DOWN, 2), (FROM_OPPOSITE, OUT, DOWN, 3),
    (ARRIVED, OUT, 2), (TERM, 0, 4), (RING, 0, DOWN, 0, 4), (RING, 0, UP, 1, 4), (TERM, 0, 5),
    (RING, 0, DOWN, 0, 5), (RING, 0, UP, 1, 5), (SEGMENT, 1), (ATTEND, 1, 0), (RING, 0, UP, 1, 1),
    (RING, 0, DOWN, 1, 3), (RING, 0, UP, 1, 2), (RING, 0, DOWN, 1, 4), (RING, 0, DOWN, 1, 5),
    (ATTEND, 1, -1), (ATTEND, 1, 1), (RING, 0, UP, 2, 3), (RING, 0, DOWN, 2, 1),
    (RING, 0, UP, 2, 4), (RING, 0, DOWN, 2, 2), (RING, 0, UP, 2, 5), (RING, 0, DOWN, 2, 3),
    (RING, 0, UP, 2, 1), (RING, 0, DOWN, 2, 4), (RING, 0, UP, 2, 2), (RING, 0, DOWN, 2, 5),
    (ATTEND, 1, 2), (CLOSE, 1), (RING, 0, UP, 3, 3), (RING, 0, DOWN, 3, 1), (RING, 0, UP, 3, 4),
    (RING, 0, DOWN, 3, 2), (RING, 0, UP, 3, 5), (RING, 0, DOWN, 3, 3), (RING, 0, UP, 3, 1),
    (RING, 0, DOWN, 3, 4), (RING, 0, UP, 3, 2), (RING, 0, DOWN, 3, 5), (TERM, 1, 1),
    (RING, 1, UP, 0, 1), (TERM, 1, 3), (RING, 1, DOWN, 0, 3), (TERM, 1, 2), (RING, 1, UP, 0, 2),
    (TERM, 1, 4), (RING, 1, DOWN, 0, 4), (TERM, 1, 5), (RING, 1, DOWN, 0, 5), (RING, 1, UP, 1, 3),
    (RING, 1, DOWN, 1, 1), (RING, 1, UP, 1, 4), (RING, 1, DOWN, 1, 2), (RING, 1, UP, 1, 5),
    (TERM, 1, 0), (ADD,), (RING, 1, UP, 0, 0), (RING, 1, DOWN, 1, 0), (RING, 1, UP, 1, 1),
    (RING, 1, DOWN, 1, 3), (RING, 1, UP, 1, 2), (RING, 1, DOWN, 1, 4), (RING, 1, DOWN, 1, 5),
    (LAST, 0, 1), (LAST, 0, 3), (LAST, 0, 2), (LAST, 0, 4), (LAST, 0, 5), (RING, 1, UP, 1, 0),
    (RING, 1, UP, 2, 3), (RING, 1, DOWN, 2, 1), (RING, 1, UP, 2, 4), (RING, 1, DOWN, 2, 2),
    (RING, 1, UP, 2, 5), (RING, 1, DOWN, 2, 0), (RING, 1, UP, 2, 1), (RING, 1, DOWN, 2, 3),
    (RING, 1, UP, 2, 2), (RING, 1, DOWN, 2, 4), (RING, 1, UP, 2, 0), (RING, 1, DOWN, 2, 5),
    (RING, 1, UP, 3, 3), (RING, 1, DOWN, 3, 1), (RING, 1, UP, 3, 4), (RING, 1, DOWN, 3, 2),
    (RING, 1, UP, 3, 5), (RING, 1, DOWN, 3, 0), (RING, 1, UP, 3, 1), (RING, 1, DOWN, 3, 3),
    (RING, 1, UP, 3, 2), (RING, 1, DOWN, 3, 4), (RING, 1, UP, 3, 0), (RING, 1, DOWN, 3, 5),
    (LAST, 1, 3), (LAST, 1, 1), (LAST, 1, 4), (LAST, 1, 2), (LAST, 1, 5), (LAST, 1, 0), (FINISH,),
)

def rope_rows(positions, head_dim):
    half = head_dim // 2
    inverse = ROPE_BASE ** (-np.arange(half, dtype=np.float64) * 2.0 / head_dim)
    angles = np.asarray(positions, np.float64)[:, None] * inverse[None, :]
    cosine, sine = np.cos(angles), np.sin(angles)
    return (
        np.concatenate([cosine, cosine], axis=1).astype(np.float32),
        np.concatenate([-sine, sine], axis=1).astype(np.float32),
    )


def unit_rms(values):
    mean_square = jnp.mean(values * values, axis=-1, keepdims=True)
    return values * lax.rsqrt(mean_square + EPSILON)


def rotate(values, cosine, signed_sine):
    half = values.shape[-1] // 2
    return values * cosine + pltpu.roll(values, half, axis=1) * signed_sine


def nt_dot(left, right):
    return lax.dot_general(left, right, (((1,), (1,)), ((), ())), preferred_element_type=F32)


def kernel(
    hid_in, ing_in, wq_in, wk_in, wv_in, qg_in, kg_in, wo_in, og_in, ck_in, cv_in, tables_in,
    table, length_ref, tool,
    out,
    hid, ing, og, qg, kg, wo, ck, tables,
    tok, wb, kvb, wob, wsrc, wst, osrc, ost, term, ru, rd, ysend, yrecv, zbuf, total,
    proj, queries, seg_keys, seg_values, attended, att_acc, row_best, row_total,
    load_sems, send_sems, recv_sems,
):
    roll, head = lax.axis_index("roll"), lax.axis_index("head")
    x, yl, c = lax.div(roll, 8), lax.rem(lax.div(roll, 2), 4), lax.rem(roll, 2)
    z, yh = lax.div(head, 2), lax.rem(head, 2)
    own_rows, width = hid.shape
    slots, shard = table.shape[0], wq_in.shape[0]
    pair = 2 * shard
    block_rows = ck.shape[0]
    hd = qg.shape[1]
    own_cache = pl.ds(pl.multiple_of(roll * block_rows, 16), block_rows)

    loads = {}

    def load(name, src, dst):
        loads[name] = pltpu.make_async_copy(src, dst, load_sems.at[len(loads)])
        loads[name].start()

    def loaded(*names):
        for name in names:
            loads[name].wait()

    load("hid", hid_in, hid)
    load("ing", ing_in, ing)
    load("wq", wq_in, wsrc.at[0])
    load("wk", wk_in, wsrc.at[1, :, pl.ds(0, hd)])
    load("wv", wv_in, wsrc.at[1, :, pl.ds(hd, hd)])
    load("ck", ck_in, ck)
    load("cv", cv_in, kvb.at[own_cache, pl.ds(hd, hd)])
    load("tables", tables_in, tables)
    load("wo", wo_in, wo)
    load("qg", qg_in, qg)
    load("kg", kg_in, kg)
    load("og", og_in, og)
    seg = tok.shape[0]
    half_width = width // 2
    piece = width // PIECES

    def wrap(value, size):
        return lax.rem(value + size, size)

    def dev(x_=x, yl_=yl, c_=c, z_=z, yh_=yh):
        return {"roll": (x_ * NY + yl_) * NC + c_, "head": z_ * NH + yh_}

    sibling = dev(c_=1 - c)
    x_up, x_down = dev(x_=wrap(x + 1, NX)), dev(x_=wrap(x - 1, NX))
    z_up, z_down = dev(z_=wrap(z + 1, NZ)), dev(z_=wrap(z - 1, NZ))
    upper = lax.div(yl, 2)
    inner = yl + upper * (3 - 2 * yl)

    def mirrored(place):
        return place + upper * (3 - 2 * place)

    y_near = [yl, mirrored(1 - inner), mirrored(2), mirrored(3)]
    y_next = dev(yl_=y_near[1])
    y_end, y_middle = dev(yl_=mirrored(0)), dev(yl_=mirrored(2))
    partner = dev(yh_=1 - yh)

    index_of = {}
    started = []

    def slot_of(key):
        return index_of.setdefault(key, len(index_of))

    def copy_of(key, src, dst, where):
        i = slot_of(key)
        return pltpu.make_async_remote_copy(
            src_ref=src, dst_ref=dst, send_sem=send_sems.at[i], recv_sem=recv_sems.at[i],
            device_id=where, device_id_type=MESH,
        )

    def send(key, src, where, dst=None, when=None):
        copy = copy_of(key, src, src if dst is None else dst, where)
        if when is None:
            copy.start()
        else:
            pl.when(when)(copy.start)
        started.append((copy, when))

    def recv(key, dst):
        copy_of(key, dst, dst, sibling).wait_recv()

    barrier = pltpu.get_barrier_semaphore()
    for where in [sibling, x_up, x_down, z_up, z_down, partner, y_next]:
        pl.semaphore_signal(barrier, inc=1, device_id=where, device_id_type=MESH)

    @pl.when(inner == 1)
    def _():
        pl.semaphore_signal(barrier, inc=1, device_id=y_middle, device_id_type=MESH)

    loaded("hid", "ing")
    normed = unit_rms(hid[...].astype(F32)) * ing[...].reshape(1, width)
    tok[pl.ds(pl.multiple_of((yh * NZ + z) * own_rows, own_rows), own_rows), :] = normed.astype(BF16)
    loaded("wq", "wk", "wv")
    pl.semaphore_wait(barrier, 7 + inner)

    send("W sibling", wsrc.at[1 - c], sibling, wst)

    def token_block(zz, yy, part):
        return tok.at[
            pl.ds(pl.multiple_of((yy * NZ + zz) * own_rows, own_rows), own_rows),
            pl.ds(part * half_width, half_width),
        ]

    def token_key(group, way, distance, part):
        return ("T", group, way, distance, part)

    def token_send(group, part):
        block = token_block(z, yh if group == 0 else 1 - yh, part)
        send(token_key(group, UP, 1, part), block, z_up)
        send(token_key(group, DOWN, 1, part), block, z_down)

    def token_own(part):
        recv(("TP", part), token_block(z, 1 - yh, part))
        token_send(1, part)

    def token_step(group, way, distance, part):
        yy = yh if group == 0 else 1 - yh
        sign, where, last = (-1, z_up, 0) if way == UP else (1, z_down, 1)
        block = token_block(wrap(z + sign * distance, NZ), yy, part)
        recv(token_key(group, way, distance, part), block)
        if distance < 3 or (distance == 3 and part == last):
            send(token_key(group, way, distance + 1, part), block, where)

    def token_partner(part):
        send(("TP", part), token_block(z, yh, part), partner)

    token_send(0, 0)
    token_send(0, 1)

    class Gather:
        def __init__(self, name, rows):
            self.name, self.rows = name, rows
            self.steps = {
                OWN_Y: self.own_y, OWN_X: self.own_x, FROM_Y: self.y_step,
                FROM_X: self.x_step, FROM_OPPOSITE: self.o_step, ARRIVED: self.arrived,
                FIRST_OWN_X: self.first_own_x, FIRST_OWN_Y: self.first_own_y,
                FIRST_FROM_X: self.first_from_x, FIRST_FROM_OPPOSITE: self.first_from_opposite,
                FIRST_FROM_Y: self.first_from_y,
            }

        def at(self, dx, i, k, core=c):
            return self.rows(wrap(x + dx, NX) * NY + y_near[i], core, k)

        def own_y(self, k):
            block = self.at(0, 0, k)
            send((self.name, "yn", k), block, y_next)
            send((self.name, "ym", 0, k), block, y_middle, when=inner == 1)

        def own_x(self, k):
            self.spread(0, k)

        def spread(self, i, k):
            block = self.at(0, i, k)
            send((self.name, UP, i, k), block, x_up)
            send((self.name, DOWN, i, k), block, x_down)
            send((self.name, "s", 0, i, k), block, sibling)

        def y_step(self, i, k):
            block = self.at(0, i, k)
            if i == 1:
                recv((self.name, "yn", k), block)
                send((self.name, "ym", 1, k), block, y_middle, when=inner == 1)
            else:
                @pl.when(inner == 1)
                def _():
                    recv((self.name, "ym", i - 2, k), block)

                @pl.when(inner == 0)
                def _():
                    recv((self.name, "ye", i, k), block)

                send((self.name, "ye", i, k), block, y_end, when=inner == 1)
            self.spread(i, k)

        def x_step(self, way, i, k):
            dx, where, last = (-1, x_up, 0) if way == UP else (1, x_down, 1)
            block = self.at(dx, i, k)
            recv((self.name, way, i, k), block)
            if k == last:
                send((self.name, "o", way, i), block, where)
            send((self.name, "s", dx, i, k), block, sibling)

        def o_step(self, way, i):
            k = 0 if way == UP else 1
            block = self.at(2, i, k)
            recv((self.name, "o", way, i), block)
            send((self.name, "s", 2, i, k), block, sibling)


        def first_y(self, dx):
            block = self.at(dx, 0, 1)
            send((self.name, "fyn", dx), block, y_next)
            send((self.name, "fym", dx, 0), block, y_middle, when=inner == 1)

        def first_own_x(self):
            block = self.at(0, 0, 1)
            send((self.name, "f", UP), block, x_up)
            send((self.name, "f", DOWN), block, x_down)
            send((self.name, "s", 0, 0, 1), block, sibling)

        def first_own_y(self):
            self.first_y(0)

        def first_from_x(self, way):
            dx, where = (-1, x_up) if way == UP else (1, x_down)
            block = self.at(dx, 0, 1)
            recv((self.name, "f", way), block)
            send((self.name, "fo", way), self.at(dx, 0, 2 + way), where)
            self.first_y(dx)
            send((self.name, "s", dx, 0, 1), block, sibling)

        def first_from_opposite(self):
            recv((self.name, "fo", UP), self.at(2, 0, 2 + UP))
            recv((self.name, "fo", DOWN), self.at(2, 0, 2 + DOWN))
            self.first_y(2)
            send((self.name, "s", 2, 0, 1), self.at(2, 0, 1), sibling)

        def first_from_y(self, dx, i):
            block = self.at(dx, i, 1)
            if i == 1:
                recv((self.name, "fyn", dx), block)
                send((self.name, "fym", dx, 1), block, y_middle, when=inner == 1)
            else:
                @pl.when(inner == 1)
                def _():
                    recv((self.name, "fym", dx, i - 2), block)

                @pl.when(inner == 0)
                def _():
                    recv((self.name, "fye", dx, i), block)

                send((self.name, "fye", dx, i), block, y_end, when=inner == 1)
            send((self.name, "s", dx, i, 1), block, sibling)

        def arrived(self, dx):
            for i in range(NY):
                for k in range(2):
                    recv((self.name, "s", dx, i, k), self.at(dx, i, k, 1 - c))

    def pair_rows(ref):
        def rows(chip, core, k):
            start, size = pair_parts[k]
            return ref.at[core, pl.ds(pl.multiple_of(chip * pair + start, 16), size)]

        return rows

    def cache_rows(chip, core, k):
        start, size = cache_parts[k]
        return kvb.at[pl.ds(pl.multiple_of((chip * NC + core) * block_rows + start, 16), size)]

    pair_parts = ((0, 176), (176, 160), (176, 80), (256, 80))
    cache_parts = ((0, 80), (80, 80), (80, 48), (128, 32))
    gathers = {
        QKV: Gather("W", pair_rows(wb)),
        CACHE: Gather("C", cache_rows),
        OUT: Gather("O", pair_rows(wob)),
    }
    chip = x * NY + yl

    def join_pair(mine, other):
        mine, other = mine.astype(F32), other.astype(F32)
        upper = jnp.where(c == 0, mine, other)
        lower = jnp.where(c == 0, other, mine)
        return jnp.concatenate([upper, lower], axis=0).astype(BF16)

    recv("W sibling", wst)
    wb[c, pl.ds(pl.multiple_of(chip * pair, 16), pair), :] = join_pair(wsrc[c], wst[...])
    for k in range(2):
        gathers[QKV].own_y(k)
        gathers[QKV].own_x(k)

    slot_block = table[roll]
    loaded("tables", "ck")
    first_seg = slots + block_rows
    block_cos, block_sin = tables[0:slots, 0:hd], tables[0:slots, hd : 2 * hd]
    row_cos, row_sin = tables[slots:first_seg, 0:hd], tables[slots:first_seg, hd : 2 * hd]
    seg_cos = tables[first_seg : first_seg + seg, 0:hd]
    seg_sin = tables[first_seg : first_seg + seg, hd : 2 * hd]
    pick = lax.broadcasted_iota(jnp.int32, (slots, hd), 0) == slot_block
    start_cos = jnp.sum(jnp.where(pick, block_cos, 0.0), axis=0, keepdims=True)
    start_sin = jnp.sum(jnp.where(pick, block_sin, 0.0), axis=0, keepdims=True)
    lane = lax.broadcasted_iota(jnp.int32, (1, hd), 1)
    sign = jnp.where(lane < hd // 2, -1.0, 1.0)
    cosine = start_cos * row_cos - start_sin * row_sin
    sine = (start_sin * row_cos + start_cos * row_sin) * sign
    kvb[own_cache, 0:hd] = rotate(ck[...].astype(F32), cosine, sine).astype(BF16)
    loaded("cv")

    loaded("wo", "qg", "kg")
    turned = wo[...]
    osrc[0] = turned[:, 0:hd]
    osrc[1] = turned[:, hd : 2 * hd]
    send("O sibling", osrc.at[1 - c], sibling, ost)

    rows = seg // NH

    def project_all():
        depth = 1792
        proj[...] = jnp.zeros_like(proj)

        def project(step, carry):
            at = pl.ds(pl.multiple_of(step * depth, depth), depth)
            tokens = tok[:, at]
            proj[:, 0 : 2 * hd] += jnp.dot(tokens, wb[0, at, :], preferred_element_type=F32)
            proj[:, 2 * hd : 4 * hd] += jnp.dot(tokens, wb[1, at, :], preferred_element_type=F32)
            return carry

        lax.fori_loop(0, width // depth, project, 0)
        for g in range(2):
            query = unit_rms(proj[:, g * hd : (g + 1) * hd]) * qg[...]
            query = rotate(query, seg_cos, seg_sin).astype(BF16)
            for yy in range(NH):
                queries[yy, g * rows : (g + 1) * rows, :] = query[yy * rows : (yy + 1) * rows]
        key = unit_rms(proj[:, 2 * hd : 3 * hd]) * kg[...]
        seg_keys[...] = rotate(key, seg_cos, seg_sin).astype(BF16)
        seg_values[...] = proj[:, 3 * hd : 4 * hd].astype(BF16)

    scale = 1.0 / QSCALE**0.5 / math.log(2.0)
    length = length_ref[0]
    group_y = (1 - yh, yh)

    def exponentials(scores, best):
        return [
            jnp.exp2((scores[:, j : j + hd] - best) * scale) for j in range(0, scores.shape[1], hd)
        ]

    def weighted(weights, values):
        weights = jnp.concatenate([part.astype(BF16) for part in weights], axis=1)
        return jnp.dot(weights, values, preferred_element_type=F32)

    def attend_segment(g):
        scores = nt_dot(queries[group_y[g]], seg_keys[...])
        row = lax.broadcasted_iota(jnp.int32, scores.shape, 0) & (rows - 1)
        row_t = row + (row >> 4) * 16 + group_y[g] * own_rows
        col = lax.broadcasted_iota(jnp.int32, scores.shape, 1)
        col_in = col & (rows - 1)
        col_t = col_in + (col_in >> 4) * 16 + (col >> 7) * own_rows
        scores = jnp.where((col_t <= row_t) & (col_t < length), scores, -1e30)
        best = jnp.broadcast_to(jnp.max(scores, axis=1, keepdims=True), row_best.shape)
        weights = exponentials(scores, best)
        row_best[...] = best
        row_total[...] = sum(weights[1:], weights[0])
        att_acc[...] = weighted(weights, seg_values[...])

    group_rows = NY * NC * block_rows

    def attend_group(g, dx):
        at = pl.ds(pl.multiple_of(wrap(x + dx, NX) * group_rows, 16), group_rows)
        scores = nt_dot(queries[group_y[g]], kvb[at, 0:hd])
        old_best = row_best[...]
        best = jnp.maximum(old_best, jnp.max(scores, axis=1, keepdims=True))
        rescale = jnp.exp2((old_best - best) * scale)
        weights = exponentials(scores, best)
        row_best[...] = best
        row_total[...] = row_total[...] * rescale + sum(weights[1:], weights[0])
        att_acc[...] = att_acc[...] * rescale + weighted(weights, kvb[at, hd : 2 * hd])

    def close_group(g):
        combined = att_acc[...] / jnp.sum(row_total[...], axis=1, keepdims=True)
        combined = combined.astype(BF16)
        for half in range(2):
            attended[g, :, half * hd : (half + 1) * hd] = combined[half * rows : (half + 1) * rows]

    x_half, x_odd = lax.div(x, 2), lax.rem(x, 2)

    def columns_of(p):
        near = x_half if p < 3 else 1 - x_half
        place = p + x_odd * (2 - 2 * p) if p < 3 else (5 - p) + x_odd * (2 * p - 8)
        return pl.ds(pl.multiple_of((near * 3 + place) * piece, 128), piece)

    def term_at(g, dz, p):
        return (
            pl.ds(
                pl.multiple_of((group_y[g] * NZ + wrap(z + dz, NZ)) * own_rows, own_rows), own_rows
            ),
            columns_of(p),
        )

    def make_term(g, p):
        at = columns_of(p)
        columns = jnp.concatenate([wob[0, at, :], wob[1, at, :]], axis=1)
        place = pl.ds(pl.multiple_of(group_y[g] * rows, rows), rows)
        term[place, at] = nt_dot(attended[g], columns).astype(BF16)

    def ring_step(g, way, k, p):
        sign, where, buf = (1, z_up, ru) if way == UP else (-1, z_down, rd)
        at = term_at(g, sign * (4 - k), p)
        first_piece = (p < PIECES // 2) == (way == UP)
        if k >= 2 or (k == 1 and first_piece):
            recv(("R", g, way, k - 1, p), buf.at[g, k - 1, p])
            term[at] = (term[at].astype(F32) + buf[g, k - 1, p].astype(F32)).astype(BF16)
        send(("R", g, way, k, p), term.at[at], where, buf.at[g, k, p])

    def swap_terms():
        place = pl.ds(pl.multiple_of(group_y[0] * rows, rows), rows)
        send(("Z",), term.at[place, columns_of(0)], partner, zbuf)

    def add_swapped():
        recv(("Z",), zbuf)
        at = (pl.ds(pl.multiple_of(group_y[1] * rows, rows), rows), columns_of(0))
        term[at] = (term[at].astype(F32) + zbuf[...].astype(F32)).astype(BF16)

    def ring_last(g, p):
        recv(("R", g, UP, 3, p), ru.at[g, 3, p])
        recv(("R", g, DOWN, 3, p), rd.at[g, 3, p])
        summed = (
            term[term_at(g, 0, p)].astype(F32)
            + ru[g, 3, p].astype(F32)
            + rd[g, 3, p].astype(F32)
        )
        if g == 0:
            ysend[p] = summed.astype(BF16)
            send(("Y", p), ysend.at[p], partner, yrecv.at[p])
        elif p == 0:
            total[:, columns_of(p)] = summed
        else:
            recv(("Y", p), yrecv.at[p])
            total[:, columns_of(p)] = summed + yrecv[p].astype(F32)

    def finish():
        loaded("og")
        branch = unit_rms(total[...]) * og[...].reshape(1, width)
        row_i = lax.broadcasted_iota(jnp.int32, (own_rows, 1), 0)
        masked = jnp.zeros((own_rows, 1), jnp.int32)
        for t in range(own_rows):
            masked = jnp.where(row_i == t, tool[0, t], masked)
        keep = jnp.where((head * own_rows + row_i < length) & (masked == 0), 1.0, 0.0)
        out[...] = ((hid[...].astype(F32) + branch) * keep).astype(BF16)

    def own_out_ready():
        recv("O sibling", ost)
        wob[c, pl.ds(pl.multiple_of(chip * pair, 16), pair), :] = join_pair(osrc[c], ost[...])

    steps = {
        TOKENS: token_step, TOKENS_SWAP: token_partner, TOKENS_OWN: token_own, READY: own_out_ready, PROJECT: project_all,
        SEGMENT: attend_segment, ATTEND: attend_group, CLOSE: close_group,
        TERM: make_term, RING: ring_step, SWAP: swap_terms, ADD: add_swapped, LAST: ring_last, FINISH: finish,
    }

    for op, *what in ORDER:
        if op in steps:
            steps[op](*what)
        else:
            gathers[what[0]].steps[op](*what[1:])

    for copy, when in started:
        if when is None:
            copy.wait_send()
        else:
            pl.when(when)(copy.wait_send)


def on_device(
    hidden, in_gain, w_query, w_key, w_value, q_gain, k_gain, w_out, out_gain,
    cache_keys, cache_values, block_table, seg_length, tool_mask,
):
    own_rows, width = hidden.shape[1:]
    hd = q_gain.shape[0]
    slots = block_table.shape[0]
    block_rows = cache_keys.shape[0]
    seg = own_rows * NZ * NH
    shard = w_query.shape[0]
    half = hd // 2
    block_cos, block_sin = rope_rows(np.arange(slots) * block_rows, hd)
    row_cos, row_sin = rope_rows(np.arange(block_rows), hd)
    block_sin = np.concatenate([block_sin[:, half:], block_sin[:, half:]], axis=1)
    row_sin = np.concatenate([row_sin[:, half:], row_sin[:, half:]], axis=1)
    tokens = np.arange(seg).reshape(NZ, NH, own_rows).transpose(1, 0, 2).reshape(-1)
    seg_cos, seg_sin = rope_rows(slots * block_rows + tokens, hd)
    tables = np.concatenate(
        [
            np.concatenate([block_cos, row_cos, seg_cos], axis=0),
            np.concatenate([block_sin, row_sin, seg_sin], axis=0),
        ],
        axis=1,
    )
    piece = width // PIECES
    vmem = pl.BlockSpec(memory_space=pltpu.VMEM)
    smem = pl.BlockSpec(memory_space=pltpu.SMEM)
    copies = 340
    result = pl.pallas_call(
        kernel,
        out_shape=jax.ShapeDtypeStruct((own_rows, width), BF16),
        in_specs=[pl.BlockSpec(memory_space=pl.ANY)] * 12 + [smem] * 3,
        out_specs=vmem,
        scratch_shapes=[
            pltpu.VMEM((own_rows, width), BF16),
            pltpu.VMEM((width,), F32),
            pltpu.VMEM((width,), F32),
            pltpu.VMEM((1, hd), F32),
            pltpu.VMEM((1, hd), F32),
            pltpu.VMEM((shard, 2 * hd), BF16),
            pltpu.VMEM((block_rows, hd), BF16),
            pltpu.VMEM(tables.shape, F32),
            pltpu.VMEM((seg, width), BF16),
            pltpu.VMEM((2, width, 2 * hd), BF16),
            pltpu.VMEM((slots * block_rows, 2 * hd), BF16),
            pltpu.VMEM((2, width, hd), BF16),
            pltpu.VMEM((2, shard, 2 * hd), BF16),
            pltpu.VMEM((shard, 2 * hd), BF16),
            pltpu.VMEM((2, shard, hd), BF16),
            pltpu.VMEM((shard, hd), BF16),
            pltpu.VMEM((seg, width), BF16),
            pltpu.VMEM((2, 4, PIECES, own_rows, piece), BF16),
            pltpu.VMEM((2, 4, PIECES, own_rows, piece), BF16),
            pltpu.VMEM((PIECES, own_rows, piece), BF16),
            pltpu.VMEM((PIECES, own_rows, piece), BF16),
            pltpu.VMEM((seg // NH, piece), BF16),
            pltpu.VMEM((own_rows, width), F32),
            pltpu.VMEM((seg, 4 * hd), F32),
            pltpu.VMEM((NH, seg, hd), BF16),
            pltpu.VMEM((seg, hd), BF16),
            pltpu.VMEM((seg, hd), BF16),
            pltpu.VMEM((2, seg // NH, 2 * hd), BF16),
            pltpu.VMEM((seg, hd), F32),
            pltpu.VMEM((seg, hd), F32),
            pltpu.VMEM((seg, hd), F32),
            pltpu.SemaphoreType.DMA((12,)),
            pltpu.SemaphoreType.DMA((copies,)),
            pltpu.SemaphoreType.DMA((copies,)),
        ],
        compiler_params=pltpu.CompilerParams(
            collective_id=0, has_side_effects=True, vmem_limit_bytes=56 * 2**20
        ),
    )(
        hidden[0], in_gain, w_query, w_key, w_value, q_gain.reshape(1, -1), k_gain.reshape(1, -1),
        w_out.T, out_gain, cache_keys, cache_values, tables,
        block_table, seg_length, tool_mask,
    )
    return result[None]


def solution(mesh):
    return jax.shard_map(
        on_device,
        mesh=mesh,
        in_specs=(
            P("roll", "head", None),
            P(),
            P("roll", "head"),
            P("roll", "head"),
            P("roll", "head"),
            P(),
            P(),
            P("head", "roll"),
            P(),
            P("roll", "head"),
            P("roll", "head"),
            P(),
            P("roll"),
            P("roll", "head"),
        ),
        out_specs=P("roll", "head", None),
        check_vma=False,
    )
```

```python
import math

import jax
import jax.numpy as jnp
import numpy as np
from jax import lax
from jax.experimental import pallas as pl
from jax.experimental.pallas import tpu as pltpu
from jax.sharding import PartitionSpec as P

QSCALE = 168
EPSILON = 1e-06
ROPE_BASE = 1000000.0
MESH = pl.DeviceIdType.MESH
F32 = jnp.float32
BF16 = jnp.bfloat16

NX, NY, NC, NZ, NH = 4, 4, 2, 8, 2
PIECES = 6

(
    TOKENS, TOKENS_SWAP, TOKENS_OWN, READY, PROJECT, SEGMENT, ATTEND, CLOSE, TERM, RING, SWAP, ADD, LAST, FINISH,
    OWN_Y, OWN_X, FROM_Y, FROM_X, FROM_OPPOSITE, ARRIVED,
    FIRST_OWN_X, FIRST_OWN_Y, FIRST_FROM_X, FIRST_FROM_OPPOSITE, FIRST_FROM_Y,
) = range(25)
UP, DOWN = range(2)
QKV, CACHE, OUT = range(3)
ORDER = (
    (READY,), (OWN_X, OUT, 0), (OWN_Y, CACHE, 0), (OWN_X, OUT, 1), (OWN_X, CACHE, 0),
    (TOKENS_SWAP, 0), (TOKENS, 0, DOWN, 1, 1), (TOKENS, 0, UP, 1, 0), (TOKENS_SWAP, 1),
    (TOKENS, 0, UP, 1, 1), (FROM_Y, QKV, 1, 0), (FROM_Y, QKV, 1, 1), (TOKENS, 0, DOWN, 1, 0),
    (OWN_Y, OUT, 1), (FROM_Y, CACHE, 1, 0), (TOKENS, 0, UP, 2, 0), (FROM_X, QKV, UP, 0, 0),
    (FROM_X, QKV, UP, 1, 0), (FIRST_OWN_X, CACHE), (FROM_X, CACHE, UP, 0, 0),
    (TOKENS, 0, DOWN, 2, 1), (FIRST_OWN_Y, CACHE), (FROM_X, QKV, DOWN, 1, 0), (TOKENS_OWN, 0),
    (TOKENS, 0, UP, 2, 1), (FROM_X, QKV, DOWN, 0, 1), (FROM_X, CACHE, DOWN, 1, 0),
    (FROM_X, QKV, DOWN, 1, 1), (FROM_Y, QKV, 2, 1), (TOKENS, 0, DOWN, 2, 0), (TOKENS_OWN, 1),
    (FROM_Y, QKV, 2, 0), (FROM_X, QKV, UP, 0, 1), (FROM_X, QKV, DOWN, 0, 0),
    (TOKENS, 1, DOWN, 1, 0), (TOKENS, 1, UP, 1, 0), (FROM_Y, QKV, 3, 0), (FROM_Y, QKV, 3, 1),
    (FIRST_FROM_Y, CACHE, 0, 1), (TOKENS, 1, UP, 1, 1), (OWN_Y, OUT, 0), (TOKENS, 1, DOWN, 1, 1),
    (FROM_Y, CACHE, 3, 0), (TOKENS, 0, DOWN, 3, 1), (FIRST_FROM_X, CACHE, DOWN),
    (TOKENS, 0, UP, 3, 0), (FIRST_FROM_X, CACHE, UP), (FROM_X, QKV, DOWN, 2, 0),
    (TOKENS, 1, UP, 2, 0), (FROM_Y, OUT, 1, 1), (FROM_X, QKV, DOWN, 2, 1), (FROM_X, OUT, UP, 0, 1),
    (FROM_OPPOSITE, QKV, UP, 1), (FROM_X, QKV, UP, 3, 0), (FROM_X, QKV, UP, 2, 0),
    (FROM_Y, CACHE, 2, 0), (TOKENS, 1, DOWN, 2, 1), (FROM_X, QKV, DOWN, 3, 1),
    (FROM_X, OUT, DOWN, 0, 1), (FIRST_FROM_Y, CACHE, 0, 3), (FROM_X, QKV, UP, 1, 1),
    (FROM_X, QKV, UP, 2, 1), (FROM_X, QKV, UP, 3, 1), (FROM_OPPOSITE, QKV, UP, 0),
    (TOKENS, 1, DOWN, 2, 0), (TOKENS, 1, UP, 2, 1), (FROM_X, CACHE, DOWN, 3, 0),
    (FROM_Y, OUT, 2, 0), (FROM_X, OUT, DOWN, 0, 0), (TOKENS, 0, DOWN, 3, 0), (FROM_Y, OUT, 2, 1),
    (FROM_Y, OUT, 1, 0), (FROM_X, QKV, DOWN, 3, 0), (FIRST_FROM_OPPOSITE, CACHE),
    (TOKENS, 1, UP, 3, 0), (FIRST_FROM_Y, CACHE, 1, 1), (FROM_OPPOSITE, QKV, DOWN, 0),
    (TOKENS, 1, DOWN, 3, 1), (FROM_Y, OUT, 3, 1), (FROM_Y, OUT, 3, 0), (FIRST_FROM_Y, CACHE, 0, 2),
    (ARRIVED, QKV, 0), (TOKENS, 0, UP, 3, 1), (FROM_X, CACHE, UP, 1, 0), (FROM_X, OUT, UP, 0, 0),
    (FROM_OPPOSITE, QKV, DOWN, 2), (TOKENS, 0, DOWN, 4, 1), (ARRIVED, OUT, 0),
    (FROM_OPPOSITE, CACHE, UP, 0), (FROM_X, CACHE, UP, 3, 0), (TOKENS, 1, UP, 3, 1),
    (FROM_OPPOSITE, QKV, UP, 3), (FROM_OPPOSITE, QKV, DOWN, 1), (FIRST_FROM_Y, CACHE, -1, 2),
    (TOKENS, 1, DOWN, 3, 0), (FROM_X, CACHE, DOWN, 0, 0), (FROM_X, CACHE, DOWN, 2, 0),
    (FROM_OPPOSITE, QKV, UP, 2), (FROM_X, OUT, DOWN, 1, 1), (ARRIVED, QKV, 1),
    (FROM_OPPOSITE, QKV, DOWN, 3), (FIRST_FROM_Y, CACHE, 2, 2), (FROM_X, OUT, UP, 1, 1),
    (FIRST_FROM_Y, CACHE, -1, 1), (ARRIVED, QKV, -1), (TOKENS, 0, UP, 4, 0),
    (TOKENS, 1, DOWN, 4, 1), (FROM_X, CACHE, UP, 2, 0), (TOKENS, 1, UP, 4, 0), (ARRIVED, QKV, 2),
    (PROJECT,), (SEGMENT, 0), (FIRST_FROM_Y, CACHE, 2, 1), (FROM_X, OUT, UP, 2, 1),
    (FIRST_FROM_Y, CACHE, 1, 3), (ARRIVED, CACHE, 0), (FIRST_FROM_Y, CACHE, -1, 3),
    (FROM_X, OUT, UP, 3, 1), (ATTEND, 0, 0), (FROM_X, OUT, DOWN, 2, 1), (FROM_X, OUT, UP, 1, 0),
    (ARRIVED, CACHE, -1), (FROM_X, OUT, DOWN, 3, 1), (FROM_X, OUT, UP, 3, 0),
    (FIRST_FROM_Y, CACHE, 1, 2), (FROM_X, OUT, DOWN, 2, 0), (FROM_X, OUT, DOWN, 1, 0),
    (FROM_OPPOSITE, OUT, DOWN, 0), (FROM_X, OUT, UP, 2, 0), (FROM_X, OUT, DOWN, 3, 0),
    (ATTEND, 0, -1), (FROM_OPPOSITE, CACHE, UP, 1), (FIRST_FROM_Y, CACHE, 2, 3),
    (FROM_OPPOSITE, CACHE, UP, 3), (ARRIVED, OUT, -1), (ARRIVED, CACHE, 1),
    (FROM_OPPOSITE, CACHE, UP, 2), (ATTEND, 0, 1), (ARRIVED, OUT, 1), (FROM_OPPOSITE, OUT, UP, 0),
    (ARRIVED, CACHE, 2), (ATTEND, 0, 2), (CLOSE, 0), (TERM, 0, 0), (SWAP,), (TERM, 0, 1),
    (RING, 0, UP, 0, 1), (RING, 0, DOWN, 1, 1), (TERM, 0, 2), (RING, 0, UP, 0, 2),
    (RING, 0, DOWN, 1, 2), (TERM, 0, 3), (RING, 0, DOWN, 0, 3), (RING, 0, UP, 1, 3),
    (FROM_OPPOSITE, OUT, UP, 3), (FROM_OPPOSITE, OUT, DOWN, 2), (FROM_OPPOSITE, OUT, DOWN, 1),
    (FROM_OPPOSITE, OUT, UP, 1), (FROM_OPPOSITE, OUT, UP, 2), (FROM_OPPOSITE, OUT, DOWN, 3),
    (ARRIVED, OUT, 2), (TERM, 0, 4), (RING, 0, DOWN, 0, 4), (RING, 0, UP, 1, 4), (TERM, 0, 5),
    (RING, 0, DOWN, 0, 5), (RING, 0, UP, 1, 5), (SEGMENT, 1), (ATTEND, 1, 0), (RING, 0, UP, 1, 1),
    (RING, 0, DOWN, 1, 3), (RING, 0, UP, 1, 2), (RING, 0, DOWN, 1, 4), (RING, 0, DOWN, 1, 5),
    (ATTEND, 1, -1), (ATTEND, 1, 1), (RING, 0, UP, 2, 3), (RING, 0, DOWN, 2, 1),
    (RING, 0, UP, 2, 4), (RING, 0, DOWN, 2, 2), (RING, 0, UP, 2, 5), (RING, 0, DOWN, 2, 3),
    (RING, 0, UP, 2, 1), (RING, 0, DOWN, 2, 4), (RING, 0, UP, 2, 2), (RING, 0, DOWN, 2, 5),
    (ATTEND, 1, 2), (CLOSE, 1), (RING, 0, UP, 3, 3), (RING, 0, DOWN, 3, 1), (RING, 0, UP, 3, 4),
    (RING, 0, DOWN, 3, 2), (RING, 0, UP, 3, 5), (RING, 0, DOWN, 3, 3), (RING, 0, UP, 3, 1),
    (RING, 0, DOWN, 3, 4), (RING, 0, UP, 3, 2), (RING, 0, DOWN, 3, 5), (TERM, 1, 1),
    (RING, 1, UP, 0, 1), (TERM, 1, 3), (RING, 1, DOWN, 0, 3), (TERM, 1, 2), (RING, 1, UP, 0, 2),
    (TERM, 1, 4), (RING, 1, DOWN, 0, 4), (TERM, 1, 5), (RING, 1, DOWN, 0, 5), (RING, 1, UP, 1, 3),
    (RING, 1, DOWN, 1, 1), (RING, 1, UP, 1, 4), (RING, 1, DOWN, 1, 2), (RING, 1, UP, 1, 5),
    (TERM, 1, 0), (ADD,), (RING, 1, UP, 0, 0), (RING, 1, DOWN, 1, 0), (RING, 1, UP, 1, 1),
    (RING, 1, DOWN, 1, 3), (RING, 1, UP, 1, 2), (RING, 1, DOWN, 1, 4), (RING, 1, DOWN, 1, 5),
    (LAST, 0, 1), (LAST, 0, 3), (LAST, 0, 2), (LAST, 0, 4), (LAST, 0, 5), (RING, 1, UP, 1, 0),
    (RING, 1, UP, 2, 3), (RING, 1, DOWN, 2, 1), (RING, 1, UP, 2, 4), (RING, 1, DOWN, 2, 2),
    (RING, 1, UP, 2, 5), (RING, 1, DOWN, 2, 0), (RING, 1, UP, 2, 1), (RING, 1, DOWN, 2, 3),
    (RING, 1, UP, 2, 2), (RING, 1, DOWN, 2, 4), (RING, 1, UP, 2, 0), (RING, 1, DOWN, 2, 5),
    (RING, 1, UP, 3, 3), (RING, 1, DOWN, 3, 1), (RING, 1, UP, 3, 4), (RING, 1, DOWN, 3, 2),
    (RING, 1, UP, 3, 5), (RING, 1, DOWN, 3, 0), (RING, 1, UP, 3, 1), (RING, 1, DOWN, 3, 3),
    (RING, 1, UP, 3, 2), (RING, 1, DOWN, 3, 4), (RING, 1, UP, 3, 0), (RING, 1, DOWN, 3, 5),
    (LAST, 1, 3), (LAST, 1, 1), (LAST, 1, 4), (LAST, 1, 2), (LAST, 1, 5), (LAST, 1, 0), (FINISH,),
)

def rope_rows(positions, head_dim):
    half = head_dim // 2
    inverse = ROPE_BASE ** (-np.arange(half, dtype=np.float64) * 2.0 / head_dim)
    angles = np.asarray(positions, np.float64)[:, None] * inverse[None, :]
    cosine, sine = np.cos(angles), np.sin(angles)
    return (
        np.concatenate([cosine, cosine], axis=1).astype(np.float32),
        np.concatenate([-sine, sine], axis=1).astype(np.float32),
    )


def unit_rms(values):
    mean_square = jnp.mean(values * values, axis=-1, keepdims=True)
    return values * lax.rsqrt(mean_square + EPSILON)


def rotate(values, cosine, signed_sine):
    half = values.shape[-1] // 2
    return values * cosine + pltpu.roll(values, half, axis=1) * signed_sine


def nt_dot(left, right):
    return lax.dot_general(left, right, (((1,), (1,)), ((), ())), preferred_element_type=F32)


def kernel(
    hid_in, ing_in, wq_in, wk_in, wv_in, qg_in, kg_in, wo_in, og_in, ck_in, cv_in, tables_in,
    table, length_ref, tool,
    out,
    hid, ing, og, qg, kg, wo, ck, tables,
    tok, wb, kvb, wob, wsrc, wst, osrc, ost, term, ru, rd, ysend, yrecv, zbuf, total,
    proj, queries, seg_keys, seg_values, attended, att_acc, row_best, row_total,
    load_sems, send_sems, recv_sems,
):
    roll, head = lax.axis_index("roll"), lax.axis_index("head")
    x, yl, c = lax.div(roll, 8), lax.rem(lax.div(roll, 2), 4), lax.rem(roll, 2)
    z, yh = lax.div(head, 2), lax.rem(head, 2)
    own_rows, width = hid.shape
    slots, shard = table.shape[0], wq_in.shape[0]
    pair = 2 * shard
    block_rows = ck.shape[0]
    hd = qg.shape[1]
    own_cache = pl.ds(pl.multiple_of(roll * block_rows, 16), block_rows)

    loads = {}

    def load(name, src, dst):
        loads[name] = pltpu.make_async_copy(src, dst, load_sems.at[len(loads)])
        loads[name].start()

    def loaded(*names):
        for name in names:
            loads[name].wait()

    load("hid", hid_in, hid)
    load("ing", ing_in, ing)
    load("wq", wq_in, wsrc.at[0])
    load("wk", wk_in, wsrc.at[1, :, pl.ds(0, hd)])
    load("wv", wv_in, wsrc.at[1, :, pl.ds(hd, hd)])
    load("ck", ck_in, ck)
    load("cv", cv_in, kvb.at[own_cache, pl.ds(hd, hd)])
    load("tables", tables_in, tables)
    load("wo", wo_in, wo)
    load("qg", qg_in, qg)
    load("kg", kg_in, kg)
    load("og", og_in, og)
    seg = tok.shape[0]
    half_width = width // 2
    piece = width // PIECES

    def wrap(value, size):
        return lax.rem(value + size, size)

    def dev(x_=x, yl_=yl, c_=c, z_=z, yh_=yh):
        return {"roll": (x_ * NY + yl_) * NC + c_, "head": z_ * NH + yh_}

    sibling = dev(c_=1 - c)
    x_up, x_down = dev(x_=wrap(x + 1, NX)), dev(x_=wrap(x - 1, NX))
    z_up, z_down = dev(z_=wrap(z + 1, NZ)), dev(z_=wrap(z - 1, NZ))
    upper = lax.div(yl, 2)
    inner = yl + upper * (3 - 2 * yl)

    def mirrored(place):
        return place + upper * (3 - 2 * place)

    y_near = [yl, mirrored(1 - inner), mirrored(2), mirrored(3)]
    y_next = dev(yl_=y_near[1])
    y_end, y_middle = dev(yl_=mirrored(0)), dev(yl_=mirrored(2))
    partner = dev(yh_=1 - yh)

    index_of = {}
    started = []

    def slot_of(key):
        return index_of.setdefault(key, len(index_of))

    def copy_of(key, src, dst, where):
        i = slot_of(key)
        return pltpu.make_async_remote_copy(
            src_ref=src, dst_ref=dst, send_sem=send_sems.at[i], recv_sem=recv_sems.at[i],
            device_id=where, device_id_type=MESH,
        )

    def send(key, src, where, dst=None, when=None):
        copy = copy_of(key, src, src if dst is None else dst, where)
        if when is None:
            copy.start()
        else:
            pl.when(when)(copy.start)
        started.append((copy, when))

    def recv(key, dst):
        copy_of(key, dst, dst, sibling).wait_recv()

    barrier = pltpu.get_barrier_semaphore()
    for where in [sibling, x_up, x_down, z_up, z_down, partner, y_next]:
        pl.semaphore_signal(barrier, inc=1, device_id=where, device_id_type=MESH)

    @pl.when(inner == 1)
    def _():
        pl.semaphore_signal(barrier, inc=1, device_id=y_middle, device_id_type=MESH)

    loaded("hid", "ing")
    normed = unit_rms(hid[...].astype(F32)) * ing[...].reshape(1, width)
    tok[pl.ds(pl.multiple_of((yh * NZ + z) * own_rows, own_rows), own_rows), :] = normed.astype(BF16)
    loaded("wq", "wk", "wv")
    pl.semaphore_wait(barrier, 7 + inner)

    send("W sibling", wsrc.at[1 - c], sibling, wst)

    def token_block(zz, yy, part):
        return tok.at[
            pl.ds(pl.multiple_of((yy * NZ + zz) * own_rows, own_rows), own_rows),
            pl.ds(part * half_width, half_width),
        ]

    def token_key(group, way, distance, part):
        return ("T", group, way, distance, part)

    def token_send(group, part):
        block = token_block(z, yh if group == 0 else 1 - yh, part)
        send(token_key(group, UP, 1, part), block, z_up)
        send(token_key(group, DOWN, 1, part), block, z_down)

    def token_own(part):
        recv(("TP", part), token_block(z, 1 - yh, part))
        token_send(1, part)

    def token_step(group, way, distance, part):
        yy = yh if group == 0 else 1 - yh
        sign, where, last = (-1, z_up, 0) if way == UP else (1, z_down, 1)
        block = token_block(wrap(z + sign * distance, NZ), yy, part)
        recv(token_key(group, way, distance, part), block)
        if distance < 3 or (distance == 3 and part == last):
            send(token_key(group, way, distance + 1, part), block, where)

    def token_partner(part):
        send(("TP", part), token_block(z, yh, part), partner)

    token_send(0, 0)
    token_send(0, 1)

    class Gather:
        def __init__(self, name, rows):
            self.name, self.rows = name, rows
            self.steps = {
                OWN_Y: self.own_y, OWN_X: self.own_x, FROM_Y: self.y_step,
                FROM_X: self.x_step, FROM_OPPOSITE: self.o_step, ARRIVED: self.arrived,
                FIRST_OWN_X: self.first_own_x, FIRST_OWN_Y: self.first_own_y,
                FIRST_FROM_X: self.first_from_x, FIRST_FROM_OPPOSITE: self.first_from_opposite,
                FIRST_FROM_Y: self.first_from_y,
            }

        def at(self, dx, i, k, core=c):
            return self.rows(wrap(x + dx, NX) * NY + y_near[i], core, k)

        def own_y(self, k):
            block = self.at(0, 0, k)
            send((self.name, "yn", k), block, y_next)
            send((self.name, "ym", 0, k), block, y_middle, when=inner == 1)

        def own_x(self, k):
            self.spread(0, k)

        def spread(self, i, k):
            block = self.at(0, i, k)
            send((self.name, UP, i, k), block, x_up)
            send((self.name, DOWN, i, k), block, x_down)
            send((self.name, "s", 0, i, k), block, sibling)

        def y_step(self, i, k):
            block = self.at(0, i, k)
            if i == 1:
                recv((self.name, "yn", k), block)
                send((self.name, "ym", 1, k), block, y_middle, when=inner == 1)
            else:
                @pl.when(inner == 1)
                def _():
                    recv((self.name, "ym", i - 2, k), block)

                @pl.when(inner == 0)
                def _():
                    recv((self.name, "ye", i, k), block)

                send((self.name, "ye", i, k), block, y_end, when=inner == 1)
            self.spread(i, k)

        def x_step(self, way, i, k):
            dx, where, last = (-1, x_up, 0) if way == UP else (1, x_down, 1)
            block = self.at(dx, i, k)
            recv((self.name, way, i, k), block)
            if k == last:
                send((self.name, "o", way, i), block, where)
            send((self.name, "s", dx, i, k), block, sibling)

        def o_step(self, way, i):
            k = 0 if way == UP else 1
            block = self.at(2, i, k)
            recv((self.name, "o", way, i), block)
            send((self.name, "s", 2, i, k), block, sibling)


        def first_y(self, dx):
            block = self.at(dx, 0, 1)
            send((self.name, "fyn", dx), block, y_next)
            send((self.name, "fym", dx, 0), block, y_middle, when=inner == 1)

        def first_own_x(self):
            block = self.at(0, 0, 1)
            send((self.name, "f", UP), block, x_up)
            send((self.name, "f", DOWN), block, x_down)
            send((self.name, "s", 0, 0, 1), block, sibling)

        def first_own_y(self):
            self.first_y(0)

        def first_from_x(self, way):
            dx, where = (-1, x_up) if way == UP else (1, x_down)
            block = self.at(dx, 0, 1)
            recv((self.name, "f", way), block)
            send((self.name, "fo", way), self.at(dx, 0, 2 + way), where)
            self.first_y(dx)
            send((self.name, "s", dx, 0, 1), block, sibling)

        def first_from_opposite(self):
            recv((self.name, "fo", UP), self.at(2, 0, 2 + UP))
            recv((self.name, "fo", DOWN), self.at(2, 0, 2 + DOWN))
            self.first_y(2)
            send((self.name, "s", 2, 0, 1), self.at(2, 0, 1), sibling)

        def first_from_y(self, dx, i):
            block = self.at(dx, i, 1)
            if i == 1:
                recv((self.name, "fyn", dx), block)
                send((self.name, "fym", dx, 1), block, y_middle, when=inner == 1)
            else:
                @pl.when(inner == 1)
                def _():
                    recv((self.name, "fym", dx, i - 2), block)

                @pl.when(inner == 0)
                def _():
                    recv((self.name, "fye", dx, i), block)

                send((self.name, "fye", dx, i), block, y_end, when=inner == 1)
            send((self.name, "s", dx, i, 1), block, sibling)

        def arrived(self, dx):
            for i in range(NY):
                for k in range(2):
                    recv((self.name, "s", dx, i, k), self.at(dx, i, k, 1 - c))

    def pair_rows(ref):
        def rows(chip, core, k):
            start, size = pair_parts[k]
            return ref.at[core, pl.ds(pl.multiple_of(chip * pair + start, 16), size)]

        return rows

    def cache_rows(chip, core, k):
        start, size = cache_parts[k]
        return kvb.at[pl.ds(pl.multiple_of((chip * NC + core) * block_rows + start, 16), size)]

    pair_parts = ((0, 176), (176, 160), (176, 80), (256, 80))
    cache_parts = ((0, 80), (80, 80), (80, 48), (128, 32))
    gathers = {
        QKV: Gather("W", pair_rows(wb)),
        CACHE: Gather("C", cache_rows),
        OUT: Gather("O", pair_rows(wob)),
    }
    chip = x * NY + yl

    def join_pair(mine, other):
        mine, other = mine.astype(F32), other.astype(F32)
        upper = jnp.where(c == 0, mine, other)
        lower = jnp.where(c == 0, other, mine)
        return jnp.concatenate([upper, lower], axis=0).astype(BF16)

    recv("W sibling", wst)
    wb[c, pl.ds(pl.multiple_of(chip * pair, 16), pair), :] = join_pair(wsrc[c], wst[...])
    for k in range(2):
        gathers[QKV].own_y(k)
        gathers[QKV].own_x(k)

    slot_block = table[roll]
    loaded("tables", "ck")
    first_seg = slots + block_rows
    block_cos, block_sin = tables[0:slots, 0:hd], tables[0:slots, hd : 2 * hd]
    row_cos, row_sin = tables[slots:first_seg, 0:hd], tables[slots:first_seg, hd : 2 * hd]
    seg_cos = tables[first_seg : first_seg + seg, 0:hd]
    seg_sin = tables[first_seg : first_seg + seg, hd : 2 * hd]
    pick = lax.broadcasted_iota(jnp.int32, (slots, hd), 0) == slot_block
    start_cos = jnp.sum(jnp.where(pick, block_cos, 0.0), axis=0, keepdims=True)
    start_sin = jnp.sum(jnp.where(pick, block_sin, 0.0), axis=0, keepdims=True)
    lane = lax.broadcasted_iota(jnp.int32, (1, hd), 1)
    sign = jnp.where(lane < hd // 2, -1.0, 1.0)
    cosine = start_cos * row_cos - start_sin * row_sin
    sine = (start_sin * row_cos + start_cos * row_sin) * sign
    kvb[own_cache, 0:hd] = rotate(ck[...].astype(F32), cosine, sine).astype(BF16)
    loaded("cv")

    loaded("wo", "qg", "kg")
    turned = wo[...]
    osrc[0] = turned[:, 0:hd]
    osrc[1] = turned[:, hd : 2 * hd]
    send("O sibling", osrc.at[1 - c], sibling, ost)

    rows = seg // NH

    def project_all():
        depth = 1792
        proj[...] = jnp.zeros_like(proj)

        def project(step, carry):
            at = pl.ds(pl.multiple_of(step * depth, depth), depth)
            tokens = tok[:, at]
            proj[:, 0 : 2 * hd] += jnp.dot(tokens, wb[0, at, :], preferred_element_type=F32)
            proj[:, 2 * hd : 4 * hd] += jnp.dot(tokens, wb[1, at, :], preferred_element_type=F32)
            return carry

        lax.fori_loop(0, width // depth, project, 0)
        for g in range(2):
            query = unit_rms(proj[:, g * hd : (g + 1) * hd]) * qg[...]
            query = rotate(query, seg_cos, seg_sin).astype(BF16)
            for yy in range(NH):
                queries[yy, g * rows : (g + 1) * rows, :] = query[yy * rows : (yy + 1) * rows]
        key = unit_rms(proj[:, 2 * hd : 3 * hd]) * kg[...]
        seg_keys[...] = rotate(key, seg_cos, seg_sin).astype(BF16)
        seg_values[...] = proj[:, 3 * hd : 4 * hd].astype(BF16)

    scale = 1.0 / QSCALE**0.5 / math.log(2.0)
    length = length_ref[0]
    group_y = (1 - yh, yh)

    def exponentials(scores, best):
        return [
            jnp.exp2((scores[:, j : j + hd] - best) * scale) for j in range(0, scores.shape[1], hd)
        ]

    def weighted(weights, values):
        weights = jnp.concatenate([part.astype(BF16) for part in weights], axis=1)
        return jnp.dot(weights, values, preferred_element_type=F32)

    def attend_segment(g):
        scores = nt_dot(queries[group_y[g]], seg_keys[...])
        row = lax.broadcasted_iota(jnp.int32, scores.shape, 0) & (rows - 1)
        row_t = row + (row >> 4) * 16 + group_y[g] * own_rows
        col = lax.broadcasted_iota(jnp.int32, scores.shape, 1)
        col_in = col & (rows - 1)
        col_t = col_in + (col_in >> 4) * 16 + (col >> 7) * own_rows
        scores = jnp.where((col_t <= row_t) & (col_t < length), scores, -1e30)
        best = jnp.broadcast_to(jnp.max(scores, axis=1, keepdims=True), row_best.shape)
        weights = exponentials(scores, best)
        row_best[...] = best
        row_total[...] = sum(weights[1:], weights[0])
        att_acc[...] = weighted(weights, seg_values[...])

    group_rows = NY * NC * block_rows

    def attend_group(g, dx):
        at = pl.ds(pl.multiple_of(wrap(x + dx, NX) * group_rows, 16), group_rows)
        scores = nt_dot(queries[group_y[g]], kvb[at, 0:hd])
        old_best = row_best[...]
        best = jnp.maximum(old_best, jnp.max(scores, axis=1, keepdims=True))
        rescale = jnp.exp2((old_best - best) * scale)
        weights = exponentials(scores, best)
        row_best[...] = best
        row_total[...] = row_total[...] * rescale + sum(weights[1:], weights[0])
        att_acc[...] = att_acc[...] * rescale + weighted(weights, kvb[at, hd : 2 * hd])

    def close_group(g):
        combined = att_acc[...] / jnp.sum(row_total[...], axis=1, keepdims=True)
        combined = combined.astype(BF16)
        for half in range(2):
            attended[g, :, half * hd : (half + 1) * hd] = combined[half * rows : (half + 1) * rows]

    x_half, x_odd = lax.div(x, 2), lax.rem(x, 2)

    def columns_of(p):
        near = x_half if p < 3 else 1 - x_half
        place = p + x_odd * (2 - 2 * p) if p < 3 else (5 - p) + x_odd * (2 * p - 8)
        return pl.ds(pl.multiple_of((near * 3 + place) * piece, 128), piece)

    def term_at(g, dz, p):
        return (
            pl.ds(
                pl.multiple_of((group_y[g] * NZ + wrap(z + dz, NZ)) * own_rows, own_rows), own_rows
            ),
            columns_of(p),
        )

    def make_term(g, p):
        at = columns_of(p)
        columns = jnp.concatenate([wob[0, at, :], wob[1, at, :]], axis=1)
        place = pl.ds(pl.multiple_of(group_y[g] * rows, rows), rows)
        term[place, at] = nt_dot(attended[g], columns).astype(BF16)

    def ring_step(g, way, k, p):
        sign, where, buf = (1, z_up, ru) if way == UP else (-1, z_down, rd)
        at = term_at(g, sign * (4 - k), p)
        first_piece = (p < PIECES // 2) == (way == UP)
        if k >= 2 or (k == 1 and first_piece):
            recv(("R", g, way, k - 1, p), buf.at[g, k - 1, p])
            term[at] = (term[at].astype(F32) + buf[g, k - 1, p].astype(F32)).astype(BF16)
        send(("R", g, way, k, p), term.at[at], where, buf.at[g, k, p])

    def swap_terms():
        place = pl.ds(pl.multiple_of(group_y[0] * rows, rows), rows)
        send(("Z",), term.at[place, columns_of(0)], partner, zbuf)

    def add_swapped():
        recv(("Z",), zbuf)
        at = (pl.ds(pl.multiple_of(group_y[1] * rows, rows), rows), columns_of(0))
        term[at] = (term[at].astype(F32) + zbuf[...].astype(F32)).astype(BF16)

    def ring_last(g, p):
        recv(("R", g, UP, 3, p), ru.at[g, 3, p])
        recv(("R", g, DOWN, 3, p), rd.at[g, 3, p])
        summed = (
            term[term_at(g, 0, p)].astype(F32)
            + ru[g, 3, p].astype(F32)
            + rd[g, 3, p].astype(F32)
        )
        if g == 0:
            ysend[p] = summed.astype(BF16)
            send(("Y", p), ysend.at[p], partner, yrecv.at[p])
        elif p == 0:
            total[:, columns_of(p)] = summed
        else:
            recv(("Y", p), yrecv.at[p])
            total[:, columns_of(p)] = summed + yrecv[p].astype(F32)

    def finish():
        loaded("og")
        branch = unit_rms(total[...]) * og[...].reshape(1, width)
        row_i = lax.broadcasted_iota(jnp.int32, (own_rows, 1), 0)
        masked = jnp.zeros((own_rows, 1), jnp.int32)
        for t in range(own_rows):
            masked = jnp.where(row_i == t, tool[0, t], masked)
        keep = jnp.where((head * own_rows + row_i < length) & (masked == 0), 1.0, 0.0)
        out[...] = ((hid[...].astype(F32) + branch) * keep).astype(BF16)

    def own_out_ready():
        recv("O sibling", ost)
        wob[c, pl.ds(pl.multiple_of(chip * pair, 16), pair), :] = join_pair(osrc[c], ost[...])

    steps = {
        TOKENS: token_step, TOKENS_SWAP: token_partner, TOKENS_OWN: token_own, READY: own_out_ready, PROJECT: project_all,
        SEGMENT: attend_segment, ATTEND: attend_group, CLOSE: close_group,
        TERM: make_term, RING: ring_step, SWAP: swap_terms, ADD: add_swapped, LAST: ring_last, FINISH: finish,
    }

    for op, *what in ORDER:
        if op in steps:
            steps[op](*what)
        else:
            gathers[what[0]].steps[op](*what[1:])

    for copy, when in started:
        if when is None:
            copy.wait_send()
        else:
            pl.when(when)(copy.wait_send)


def on_device(
    hidden, in_gain, w_query, w_key, w_value, q_gain, k_gain, w_out, out_gain,
    cache_keys, cache_values, block_table, seg_length, tool_mask,
):
    own_rows, width = hidden.shape[1:]
    hd = q_gain.shape[0]
    slots = block_table.shape[0]
    block_rows = cache_keys.shape[0]
    seg = own_rows * NZ * NH
    shard = w_query.shape[0]
    half = hd // 2
    block_cos, block_sin = rope_rows(np.arange(slots) * block_rows, hd)
    row_cos, row_sin = rope_rows(np.arange(block_rows), hd)
    block_sin = np.concatenate([block_sin[:, half:], block_sin[:, half:]], axis=1)
    row_sin = np.concatenate([row_sin[:, half:], row_sin[:, half:]], axis=1)
    tokens = np.arange(seg).reshape(NZ, NH, own_rows).transpose(1, 0, 2).reshape(-1)
    seg_cos, seg_sin = rope_rows(slots * block_rows + tokens, hd)
    tables = np.concatenate(
        [
            np.concatenate([block_cos, row_cos, seg_cos], axis=0),
            np.concatenate([block_sin, row_sin, seg_sin], axis=0),
        ],
        axis=1,
    )
    piece = width // PIECES
    vmem = pl.BlockSpec(memory_space=pltpu.VMEM)
    smem = pl.BlockSpec(memory_space=pltpu.SMEM)
    copies = 340
    result = pl.pallas_call(
        kernel,
        out_shape=jax.ShapeDtypeStruct((own_rows, width), BF16),
        in_specs=[pl.BlockSpec(memory_space=pl.ANY)] * 12 + [smem] * 3,
        out_specs=vmem,
        scratch_shapes=[
            pltpu.VMEM((own_rows, width), BF16),
            pltpu.VMEM((width,), F32),
            pltpu.VMEM((width,), F32),
            pltpu.VMEM((1, hd), F32),
            pltpu.VMEM((1, hd), F32),
            pltpu.VMEM((shard, 2 * hd), BF16),
            pltpu.VMEM((block_rows, hd), BF16),
            pltpu.VMEM(tables.shape, F32),
            pltpu.VMEM((seg, width), BF16),
            pltpu.VMEM((2, width, 2 * hd), BF16),
            pltpu.VMEM((slots * block_rows, 2 * hd), BF16),
            pltpu.VMEM((2, width, hd), BF16),
            pltpu.VMEM((2, shard, 2 * hd), BF16),
            pltpu.VMEM((shard, 2 * hd), BF16),
            pltpu.VMEM((2, shard, hd), BF16),
            pltpu.VMEM((shard, hd), BF16),
            pltpu.VMEM((seg, width), BF16),
            pltpu.VMEM((2, 4, PIECES, own_rows, piece), BF16),
            pltpu.VMEM((2, 4, PIECES, own_rows, piece), BF16),
            pltpu.VMEM((PIECES, own_rows, piece), BF16),
            pltpu.VMEM((PIECES, own_rows, piece), BF16),
            pltpu.VMEM((seg // NH, piece), BF16),
            pltpu.VMEM((own_rows, width), F32),
            pltpu.VMEM((seg, 4 * hd), F32),
            pltpu.VMEM((NH, seg, hd), BF16),
            pltpu.VMEM((seg, hd), BF16),
            pltpu.VMEM((seg, hd), BF16),
            pltpu.VMEM((2, seg // NH, 2 * hd), BF16),
            pltpu.VMEM((seg, hd), F32),
            pltpu.VMEM((seg, hd), F32),
            pltpu.VMEM((seg, hd), F32),
            pltpu.SemaphoreType.DMA((12,)),
            pltpu.SemaphoreType.DMA((copies,)),
            pltpu.SemaphoreType.DMA((copies,)),
        ],
        compiler_params=pltpu.CompilerParams(
            collective_id=0, has_side_effects=True, vmem_limit_bytes=56 * 2**20
        ),
    )(
        hidden[0], in_gain, w_query, w_key, w_value, q_gain.reshape(1, -1), k_gain.reshape(1, -1),
        w_out.T, out_gain, cache_keys, cache_values, tables,
        block_table, seg_length, tool_mask,
    )
    return result[None]


def solution(mesh):
    return jax.shard_map(
        on_device,
        mesh=mesh,
        in_specs=(
            P("roll", "head", None),
            P(),
            P("roll", "head"),
            P("roll", "head"),
            P("roll", "head"),
            P(),
            P(),
            P("head", "roll"),
            P(),
            P("roll", "head"),
            P("roll", "head"),
            P(),
            P("roll"),
            P("roll", "head"),
        ),
        out_specs=P("roll", "head", None),
        check_vma=False,
    )
```
